32 devices in a mesh: row: 4 (over y, x), col: 8 (over z, core).
Axes of the slice: x: 2, y: 2, z: 4, core: 2. Of those that a mesh axis runs over, the one named last changes fastest.
Arguments:
- fields: float32 [5, 1, 128, 2048], P(None, None, 'col', 'row'), may hold values from -3 to 150, as said below
Outputs:
- updated: float32 [5, 1, 128, 2048], P(None, None, 'col', 'row')
The draws below stay inside these ranges and needn't reach their ends.
Inputs may be any that keep to these rules, and one draw needn't show every extreme that they name: `fields`: field 0 is the density and field 4 the total energy; density and pressure are positive in every cell.
All inputs are finite; a program needn't handle non-finite values.
Results may differ from the reference program's by a relative error of at most 0.0003.
Values sent between devices are 32-bit elements; how exact they have to be, the bound alone decides.
A program may use at most 64 MiB of HBM per device.

```python
import jax
import jax.numpy as jnp
from jax import lax

NX = 2048
SLAB = 1
NY = 128


GAMMA = 1.4


BUBBLE_RADIUS = 12.0


def draw_fields(key, part):
    keys = jax.random.split(key, 9)
    shape_three = (SLAB, NY, NX)
    column_cell = jnp.arange(NX, dtype=jnp.float32)[None, None, :]
    row_cell = jnp.arange(NY, dtype=jnp.float32)[None, :, None]
    column_pos = column_cell / NX
    row_pos = row_cell / NY
    ramp = 1.0 + 4.0 * column_pos + 4.0 * row_pos
    centre_x = jax.random.uniform(keys[5], (), jnp.float32, 0.25, 0.75) * NX
    centre_y = jax.random.uniform(keys[6], (), jnp.float32, 0.1, 0.9) * NY
    heating = jax.random.uniform(keys[7], (), jnp.float32, 10.0, 16.0)
    dilution = jax.random.uniform(keys[8], (), jnp.float32, 2.0, 3.0)
    offset_x = column_cell - centre_x
    offset_y = row_cell - centre_y
    bubble = jnp.exp(-(offset_x * offset_x + offset_y * offset_y) / (BUBBLE_RADIUS * BUBBLE_RADIUS))
    density = jax.random.uniform(keys[0], shape_three, jnp.float32, 1.0, 2.0)
    velocity_x = jax.random.uniform(keys[1], shape_three, jnp.float32, -0.5, 0.5)
    velocity_y = jax.random.uniform(keys[2], shape_three, jnp.float32, -0.5, 0.5)
    velocity_z = jax.random.uniform(keys[3], shape_three, jnp.float32, -0.5, 0.5)
    base_pressure = jax.random.uniform(keys[4], shape_three, jnp.float32, 1.0, 2.0)
    density = density / (1.0 + dilution * bubble)
    pressure = base_pressure * (ramp + heating * bubble)
    speed_square = velocity_x * velocity_x + velocity_y * velocity_y + velocity_z * velocity_z
    energy = pressure / (GAMMA - 1.0) + 0.5 * density * speed_square
    return jnp.stack([density, density * velocity_x, density * velocity_y, density * velocity_z, energy])


def setup_inputs(seed: int = 0) -> dict:
    splits = jax.random.split(jax.random.key(seed), 2)
    return {
        "fields": draw_fields(jax.random.fold_in(splits[1], 71), 0),
    }


GAMMA = 1.4
COURANT = 0.3

def window_slice(profile, begin_at, trim_end, direction_axis):
    direction_axis = direction_axis % profile.ndim
    return lax.slice_in_dim(profile, begin_at, profile.shape[direction_axis] - trim_end, axis=direction_axis)

def minmod(first_slope, second_slope):
    return 0.5 * (jnp.sign(first_slope) + jnp.sign(second_slope)) * jnp.minimum(jnp.abs(first_slope), jnp.abs(second_slope))

def rebuild(profile, direction_axis):
    far_left = window_slice(profile, 0, 3, direction_axis)
    near_left = window_slice(profile, 1, 2, direction_axis)
    near_right = window_slice(profile, 2, 1, direction_axis)
    far_right = window_slice(profile, 3, 0, direction_axis)
    edge_value = 7.0 / 12.0 * (near_left + near_right) - 1.0 / 12.0 * (far_left + far_right)
    edge_value = jnp.clip(edge_value, jnp.minimum(near_left, near_right), jnp.maximum(near_left, near_right))
    centre = window_slice(profile, 2, 2, direction_axis)
    lower_edge = window_slice(edge_value, 0, 1, direction_axis)
    upper_edge = window_slice(edge_value, 1, 0, direction_axis)
    upper_jump = upper_edge - centre
    lower_jump = centre - lower_edge
    right_face = centre + minmod(upper_jump, 2.0 * lower_jump)
    left_face = centre - minmod(lower_jump, 2.0 * upper_jump)
    return (window_slice(right_face, 0, 1, direction_axis), window_slice(left_face, 1, 0, direction_axis))

def face_terms(density, velocity, pressure, normal):
    speed_square = velocity[0] * velocity[0] + velocity[1] * velocity[1] + velocity[2] * velocity[2]
    energy = pressure / (GAMMA - 1.0) + 0.5 * density * speed_square
    normal_speed = velocity[normal - 1]
    conserved = [density, density * velocity[0], density * velocity[1], density * velocity[2], energy]
    face_flux = [density * normal_speed]
    for component in range(3):
        momentum_flux = density * normal_speed * velocity[component]
        if component == normal - 1:
            momentum_flux = momentum_flux + pressure
        face_flux.append(momentum_flux)
    face_flux.append(normal_speed * (energy + pressure))
    signal = jnp.abs(normal_speed) + jnp.sqrt(GAMMA * pressure / density)
    return (conserved, face_flux, signal)

def primitives(cells):
    density = cells[0]
    velocity = [cells[1] / density, cells[2] / density, cells[3] / density]
    kinetic = 0.5 * density * (velocity[0] * velocity[0] + velocity[1] * velocity[1] + velocity[2] * velocity[2])
    pressure = (GAMMA - 1.0) * (cells[4] - kinetic)
    return (density, velocity, pressure)

def courant(cells):
    density, velocity, pressure = primitives(cells)
    return jnp.maximum(jnp.abs(velocity[0]), jnp.abs(velocity[1])) + jnp.sqrt(GAMMA * pressure / density)

def sweep_along(padded, time_step, direction_axis, normal):
    density, velocity, pressure = primitives(padded)
    face_pairs = [rebuild(profile, direction_axis) for profile in [density, velocity[0], velocity[1], velocity[2], pressure]]
    left_states = [pair[0] for pair in face_pairs]
    right_states = [pair[1] for pair in face_pairs]
    left_conserved, left_flux, left_signal = face_terms(left_states[0], left_states[1:4], left_states[4], normal)
    right_conserved, right_flux, right_signal = face_terms(right_states[0], right_states[1:4], right_states[4], normal)
    signal = jnp.maximum(left_signal, right_signal)
    results = []
    for component in range(5):
        face_flux = 0.5 * (left_flux[component] + right_flux[component]) - 0.5 * signal * (right_conserved[component] - left_conserved[component])
        difference = window_slice(face_flux, 1, 0, direction_axis) - window_slice(face_flux, 0, 1, direction_axis)
        results.append(window_slice(padded[component], 3, 3, direction_axis) - time_step * difference)
    return jnp.stack(results)

def reference(fields):
    planes = jnp.moveaxis(fields, 1, 0)
    peak_speed = jnp.max(lax.map(lambda slab_plane: jnp.max(courant(slab_plane)), planes))
    time_step = COURANT / peak_speed

    def advance(slab_plane):
        padded = jnp.concatenate([slab_plane[..., -3:], slab_plane, slab_plane[..., :3]], axis=-1)
        halfway = sweep_along(padded, time_step, -1, 1)
        padded = jnp.concatenate([halfway[..., -3:, :], halfway, halfway[..., :3, :]], axis=-2)
        return sweep_along(padded, time_step, -2, 2)
    result = lax.map(advance, planes)
    return jnp.moveaxis(result, 0, 1)
```

```python
import functools

import jax
import jax.numpy as jnp
from jax import lax
from jax.experimental import pallas as pl
from jax.experimental.pallas import tpu as pltpu
from jax.sharding import PartitionSpec as P

GAMMA = 1.4
COURANT = 0.3
MESH = pl.DeviceIdType.MESH
LANES = 128
SUBLANES = 8
TINY = 1e-37


def inverse(value):
    guess = pl.reciprocal(value, approx=True)
    return guess * (2.0 - value * guess)


def root(value):
    return value * lax.rsqrt(jnp.maximum(value, TINY))


def primitives(cells):
    density = cells[0]
    inverse_density = inverse(density)
    velocity = [cells[k] * inverse_density for k in (1, 2, 3)]
    square = velocity[0] * velocity[0] + velocity[1] * velocity[1] + velocity[2] * velocity[2]
    pressure = (GAMMA - 1.0) * (cells[4] - 0.5 * density * square)
    return [density] + velocity + [pressure], inverse_density


def limited(first, second):
    return jnp.minimum(jnp.maximum(first, jnp.minimum(second, 0.0)), jnp.maximum(second, 0.0))


def face_values(q, up, down):
    after = up(q)
    edge = 7.0 / 12.0 * (q + after) - 1.0 / 12.0 * (down(q) + up(after))
    edge = jnp.minimum(jnp.maximum(edge, jnp.minimum(q, after)), jnp.maximum(q, after))
    rise = edge - q
    fall = q - down(edge)
    right = q + limited(rise, fall + fall)
    left = q - limited(fall, rise + rise)
    return right, up(left)


def face_terms(state, normal):
    density, pressure = state[0], state[4]
    velocity = state[1:4]
    square = velocity[0] * velocity[0] + velocity[1] * velocity[1] + velocity[2] * velocity[2]
    energy = pressure * (1.0 / (GAMMA - 1.0)) + 0.5 * density * square
    speed = velocity[normal - 1]
    momentum = [density * v for v in velocity]
    mass_flux = momentum[normal - 1]
    flux = [mass_flux] + [mass_flux * v for v in velocity] + [speed * (energy + pressure)]
    flux[normal] = flux[normal] + pressure
    signal = jnp.abs(speed) + root(GAMMA * pressure * inverse(density))
    return [density] + momentum + [energy], flux, signal


def flux_differences(profiles, up, down, normal):
    pairs = [face_values(q, up, down) for q in profiles]
    left_cons, left_flux, left_signal = face_terms([a for a, _ in pairs], normal)
    right_cons, right_flux, right_signal = face_terms([b for _, b in pairs], normal)
    signal = jnp.maximum(left_signal, right_signal)
    results = []
    for k in range(5):
        flux = (left_flux[k] + right_flux[k]) - signal * (right_cons[k] - left_cons[k])
        results.append(flux - down(flux))
    return results


def shifts(length, axis):
    return (
        lambda a: pltpu.roll(a, length - 1, axis),
        lambda a: pltpu.roll(a, 1, axis),
    )


def kernel(
    rows, cols, x, out, u, df, prim, xr, xl, yt, yb, rxl, rxr, rya, ryb, rc, m0, m1, m1s, m2,
    in_sem, halo_send, halo_recv, row_send, row_recv, col_send, col_recv,
):
    ny, nx = x.shape[2], x.shape[3]
    me_r, me_c = lax.axis_index("row"), lax.axis_index("col")

    def row_at(step):
        return lax.rem(me_r + (step % rows), rows)

    def col_at(step):
        return lax.rem(me_c + (step % cols), cols)

    load = pltpu.make_async_copy(x.at[:, 0], u.at[:, pl.ds(0, ny)], in_sem)
    load.start()

    barrier = pltpu.get_barrier_semaphore()
    peers = [(row_at(d), me_c) for d in range(1, rows)]
    peers += [(me_r, col_at(d)) for d in range(1, cols)]
    peers += [(row_at(a), col_at(b)) for a in (1, -1) for b in (1, -1)]
    for peer in peers:
        pl.semaphore_signal(barrier, inc=1, device_id=peer, device_id_type=MESH)
    load.wait()

    peak = None
    for r in range(0, ny, SUBLANES):
        profiles, inverse_density = primitives([u[f, r : r + SUBLANES, :] for f in range(5)])
        for f in range(5):
            prim[f, r : r + SUBLANES, :] = profiles[f]
        speed = jnp.maximum(jnp.abs(profiles[1]), jnp.abs(profiles[2]))
        speed = speed + root(GAMMA * profiles[4] * inverse_density)
        for c in range(0, nx, LANES):
            part = speed[:, c : c + LANES]
            peak = part if peak is None else jnp.maximum(peak, part)
    m0[...] = peak
    pl.semaphore_wait(barrier, len(peers))

    sends = []

    def send(src, dst, send_sem, recv_sem, device):
        copy = pltpu.make_async_remote_copy(
            src_ref=src, dst_ref=dst, send_sem=send_sem, recv_sem=recv_sem,
            device_id=device, device_id_type=MESH,
        )
        copy.start()
        sends.append(copy)
        return copy

    for d in range(1, rows):
        send(m0, m1.at[d - 1], row_send.at[d - 1], row_recv, (row_at(d), me_c))

    lane = lax.broadcasted_iota(jnp.int32, (ny, LANES), 1)
    pack_r = pack_l = None
    for f in range(5):
        edge_r = pltpu.roll(u[f, 0:ny, nx - LANES : nx], 8 * f + 3, 1)
        edge_l = u[f, 0:ny, 0:LANES]
        if f:
            edge_l = pltpu.roll(edge_l, 8 * f, 1)
            pack_r = jnp.where(lane < 8 * f, pack_r, edge_r)
            pack_l = jnp.where(lane < 8 * f, pack_l, edge_l)
        else:
            pack_r, pack_l = edge_r, edge_l
    xr[...] = pack_r
    xl[...] = pack_l
    for f in range(5):
        yt[3 * f : 3 * f + 3, :] = u[f, 0:3, :]
        yb[3 * f : 3 * f + 3, :] = u[f, ny - 3 : ny, :]
    yt[15:16, :] = u[0, 0:1, :]
    yb[15:16, :] = u[0, 0:1, :]
    top, bottom = pl.ds(0, SUBLANES), pl.ds(ny - SUBLANES, SUBLANES)
    halos = []
    for i, (src, dst, device) in enumerate(
        [
            (yb, rya, (me_r, col_at(1))),
            (yt, ryb, (me_r, col_at(-1))),
            (xr, rxl, (row_at(1), me_c)),
            (xl, rxr, (row_at(-1), me_c)),
            (xr.at[bottom], rc.at[0], (row_at(1), col_at(1))),
            (xl.at[bottom], rc.at[1], (row_at(-1), col_at(1))),
            (xr.at[top], rc.at[2], (row_at(1), col_at(-1))),
            (xl.at[top], rc.at[3], (row_at(-1), col_at(-1))),
        ]
    ):
        halos.append(send(src, dst, halo_send.at[i], halo_recv.at[i], device))

    pltpu.make_async_copy(m1, m1, row_recv).wait()
    peak = m0[...]
    for d in range(rows - 1):
        peak = jnp.maximum(peak, m1[d])
    m1s[...] = peak
    for d in range(1, cols):
        send(m1s, m2.at[d - 1], col_send.at[d - 1], col_recv, (me_r, col_at(d)))

    up, down = shifts(nx, 1)
    for r in range(0, ny, SUBLANES):
        profiles = [prim[f, r : r + SUBLANES, :] for f in range(5)]
        for f, difference in enumerate(flux_differences(profiles, up, down, 1)):
            df[f, r : r + SUBLANES, :] = difference

    halos[0].wait_recv()
    halos[1].wait_recv()
    for f in range(5):
        u[f, ny : ny + 3, :] = ryb[3 * f : 3 * f + 3, :]
        u[f, ny + 3 : ny + 5, :] = u[f, 3:5, :]
        u[f, ny + 5 : ny + 8, :] = rya[3 * f : 3 * f + 3, :]
    profiles, _ = primitives([u[f, ny : ny + SUBLANES, :] for f in range(5)])
    for f, difference in enumerate(flux_differences(profiles, up, down, 1)):
        df[f, ny : ny + SUBLANES, :] = difference

    for copy in halos[2:]:
        copy.wait_recv()
    total = ny + SUBLANES
    lane = lax.broadcasted_iota(jnp.int32, (total, LANES), 1)
    below = lax.broadcasted_iota(jnp.int32, (SUBLANES, LANES), 0) < 4
    far_left = jnp.concatenate([rxl[...], jnp.where(below, rc[2], rc[0])], axis=0)
    far_right = jnp.concatenate([rxr[...], jnp.where(below, rc[3], rc[1])], axis=0)
    seam = []
    for f in range(5):
        begin = u[f, :, 0:LANES]
        end = pltpu.roll(u[f, :, nx - LANES : nx], 64, 1)
        before = pltpu.roll(far_left, 125 - 8 * f, 1)
        after = pltpu.roll(far_right, 64 - 8 * f, 1)
        tile = jnp.where(lane < 32, begin, end)
        tile = jnp.where(lane >= 125, before, tile)
        seam.append(jnp.where((lane >= 64) & (lane < 67), after, tile))
    profiles, _ = primitives(seam)
    up, down = shifts(LANES, 1)
    for f, difference in enumerate(flux_differences(profiles, up, down, 1)):
        df[f, :, 0:LANES] = jnp.where(lane < 3, difference, df[f, :, 0:LANES])
        df[f, :, nx - LANES : nx] = jnp.where(
            lane >= 125, pltpu.roll(difference, 64, 1), df[f, :, nx - LANES : nx]
        )

    pltpu.make_async_copy(m2, m2, col_recv).wait()
    for d in range(cols - 1):
        peak = jnp.maximum(peak, m2[d])
    peak = jnp.max(jnp.max(peak, axis=0, keepdims=True), axis=1, keepdims=True)
    half_step = (0.5 * COURANT) / peak

    up, down = shifts(total, 0)
    for c in range(0, nx, LANES):
        cells = [
            u[f, :, c : c + LANES] - half_step * df[f, :, c : c + LANES] for f in range(5)
        ]
        profiles, _ = primitives(cells)
        for f, difference in enumerate(flux_differences(profiles, up, down, 2)):
            result = cells[f] - half_step * difference
            out[f, 0, :, c : c + LANES] = result[0:ny]

    for copy in sends:
        copy.wait_send()


def local(rows, cols, fields):
    ny, nx = fields.shape[2], fields.shape[3]
    vmem = lambda *shape: pltpu.VMEM(shape, jnp.float32)
    dma = pltpu.SemaphoreType.DMA
    return pl.pallas_call(
        functools.partial(kernel, rows, cols),
        out_shape=jax.ShapeDtypeStruct(fields.shape, fields.dtype),
        in_specs=[pl.BlockSpec(memory_space=pl.ANY)],
        out_specs=pl.BlockSpec(memory_space=pltpu.VMEM),
        scratch_shapes=[
            vmem(5, ny + SUBLANES, nx),
            vmem(5, ny + SUBLANES, nx),
            vmem(5, ny, nx),
            vmem(ny, LANES),
            vmem(ny, LANES),
            vmem(16, nx),
            vmem(16, nx),
            vmem(ny, LANES),
            vmem(ny, LANES),
            vmem(16, nx),
            vmem(16, nx),
            vmem(4, SUBLANES, LANES),
            vmem(SUBLANES, LANES),
            vmem(rows - 1, SUBLANES, LANES),
            vmem(SUBLANES, LANES),
            vmem(cols - 1, SUBLANES, LANES),
            dma,
            dma((8,)),
            dma((8,)),
            dma((rows - 1,)),
            dma,
            dma((cols - 1,)),
            dma,
        ],
        compiler_params=pltpu.CompilerParams(
            collective_id=0, has_side_effects=True, vmem_limit_bytes=32 * 1024 * 1024
        ),
        name="sweeps",
    )(fields)


def solution(mesh):
    spec = P(None, None, "col", "row")
    return jax.shard_map(
        functools.partial(local, mesh.shape["row"], mesh.shape["col"]),
        mesh=mesh,
        in_specs=(spec,),
        out_specs=spec,
        check_vma=False,
    )
```

```python
import functools

import jax
import jax.numpy as jnp
from jax import lax
from jax.experimental import pallas as pl
from jax.experimental.pallas import tpu as pltpu
from jax.sharding import PartitionSpec as P

GAMMA = 1.4
COURANT = 0.3
MESH = pl.DeviceIdType.MESH
LANES = 128
SUBLANES = 8
TINY = 1e-37


def inverse(value):
    guess = pl.reciprocal(value, approx=True)
    return guess * (2.0 - value * guess)


def root(value):
    return value * lax.rsqrt(jnp.maximum(value, TINY))


def primitives(cells):
    density = cells[0]
    inverse_density = inverse(density)
    velocity = [cells[k] * inverse_density for k in (1, 2, 3)]
    square = velocity[0] * velocity[0] + velocity[1] * velocity[1] + velocity[2] * velocity[2]
    pressure = (GAMMA - 1.0) * (cells[4] - 0.5 * density * square)
    return [density] + velocity + [pressure], inverse_density


def limited(first, second):
    return jnp.minimum(jnp.maximum(first, jnp.minimum(second, 0.0)), jnp.maximum(second, 0.0))


def face_values(q, up, down):
    after = up(q)
    edge = 7.0 / 12.0 * (q + after) - 1.0 / 12.0 * (down(q) + up(after))
    edge = jnp.minimum(jnp.maximum(edge, jnp.minimum(q, after)), jnp.maximum(q, after))
    rise = edge - q
    fall = q - down(edge)
    right = q + limited(rise, fall + fall)
    left = q - limited(fall, rise + rise)
    return right, up(left)


def face_terms(state, normal):
    density, pressure = state[0], state[4]
    velocity = state[1:4]
    square = velocity[0] * velocity[0] + velocity[1] * velocity[1] + velocity[2] * velocity[2]
    energy = pressure * (1.0 / (GAMMA - 1.0)) + 0.5 * density * square
    speed = velocity[normal - 1]
    momentum = [density * v for v in velocity]
    mass_flux = momentum[normal - 1]
    flux = [mass_flux] + [mass_flux * v for v in velocity] + [speed * (energy + pressure)]
    flux[normal] = flux[normal] + pressure
    signal = jnp.abs(speed) + root(GAMMA * pressure * inverse(density))
    return [density] + momentum + [energy], flux, signal


def flux_differences(profiles, up, down, normal):
    pairs = [face_values(q, up, down) for q in profiles]
    left_cons, left_flux, left_signal = face_terms([a for a, _ in pairs], normal)
    right_cons, right_flux, right_signal = face_terms([b for _, b in pairs], normal)
    signal = jnp.maximum(left_signal, right_signal)
    results = []
    for k in range(5):
        flux = (left_flux[k] + right_flux[k]) - signal * (right_cons[k] - left_cons[k])
        results.append(flux - down(flux))
    return results


def shifts(length, axis):
    return (
        lambda a: pltpu.roll(a, length - 1, axis),
        lambda a: pltpu.roll(a, 1, axis),
    )


def kernel(
    rows, cols, x, out, u, df, prim, xr, xl, yt, yb, rxl, rxr, rya, ryb, rc, mine, others,
    in_sem, halo_send, halo_recv, peak_send, peak_recv,
):
    ny, nx = x.shape[2], x.shape[3]
    me_r, me_c = lax.axis_index("row"), lax.axis_index("col")

    def row_at(step):
        return lax.rem(me_r + (step % rows), rows)

    def col_at(step):
        return lax.rem(me_c + (step % cols), cols)

    load = pltpu.make_async_copy(x.at[:, 0], u.at[:, pl.ds(0, ny)], in_sem)
    load.start()

    barrier = pltpu.get_barrier_semaphore()
    count = rows * cols

    def peer(d):
        return lax.rem(me_r + d // cols, rows), lax.rem(me_c + d % cols, cols)

    @pl.loop(1, count)
    def _(d):
        pl.semaphore_signal(barrier, inc=1, device_id=peer(d), device_id_type=MESH)

    load.wait()

    peak = None
    for r in range(0, ny, SUBLANES):
        profiles, inverse_density = primitives([u[f, r : r + SUBLANES, :] for f in range(5)])
        for f in range(5):
            prim[f, r : r + SUBLANES, :] = profiles[f]
        speed = jnp.maximum(jnp.abs(profiles[1]), jnp.abs(profiles[2]))
        speed = speed + root(GAMMA * profiles[4] * inverse_density)
        for c in range(0, nx, LANES):
            part = speed[:, c : c + LANES]
            peak = part if peak is None else jnp.maximum(peak, part)
    mine[...] = jnp.max(peak, axis=0, keepdims=True)

    lane = lax.broadcasted_iota(jnp.int32, (ny, LANES), 1)
    pack_r = pack_l = None
    for f in range(5):
        edge_r = pltpu.roll(u[f, 0:ny, nx - LANES : nx], 8 * f + 3, 1)
        edge_l = u[f, 0:ny, 0:LANES]
        if f:
            edge_l = pltpu.roll(edge_l, 8 * f, 1)
            pack_r = jnp.where(lane < 8 * f, pack_r, edge_r)
            pack_l = jnp.where(lane < 8 * f, pack_l, edge_l)
        else:
            pack_r, pack_l = edge_r, edge_l
    xr[...] = pack_r
    xl[...] = pack_l
    for f in range(5):
        yt[3 * f : 3 * f + 3, :] = u[f, 0:3, :]
        yb[3 * f : 3 * f + 3, :] = u[f, ny - 3 : ny, :]
    yt[15:16, :] = u[0, 0:1, :]
    yb[15:16, :] = u[0, 0:1, :]
    up, down = shifts(nx, 1)
    for r in range(0, ny, SUBLANES):
        profiles = [prim[f, r : r + SUBLANES, :] for f in range(5)]
        for f, difference in enumerate(flux_differences(profiles, up, down, 1)):
            df[f, r : r + SUBLANES, :] = difference

    pl.semaphore_wait(barrier, count - 1)
    top, bottom = pl.ds(0, SUBLANES), pl.ds(ny - SUBLANES, SUBLANES)
    halos = []
    for i, (src, dst, device) in enumerate(
        [
            (yb, rya, (me_r, col_at(1))),
            (yt, ryb, (me_r, col_at(-1))),
            (xr, rxl, (row_at(1), me_c)),
            (xl, rxr, (row_at(-1), me_c)),
            (xr.at[bottom], rc.at[0], (row_at(1), col_at(1))),
            (xl.at[bottom], rc.at[1], (row_at(-1), col_at(1))),
            (xr.at[top], rc.at[2], (row_at(1), col_at(-1))),
            (xl.at[top], rc.at[3], (row_at(-1), col_at(-1))),
        ]
    ):
        halos.append(
            pltpu.make_async_remote_copy(
                src_ref=src, dst_ref=dst, send_sem=halo_send.at[i], recv_sem=halo_recv.at[i],
                device_id=device, device_id_type=MESH,
            )
        )
        halos[i].start()


    @pl.loop(1, count)
    def _(d):
        pltpu.make_async_remote_copy(
            src_ref=mine, dst_ref=others.at[d - 1], send_sem=peak_send, recv_sem=peak_recv,
            device_id=peer(d), device_id_type=MESH,
        ).start()

    halos[0].wait_recv()
    halos[1].wait_recv()
    for f in range(5):
        u[f, ny : ny + 3, :] = ryb[3 * f : 3 * f + 3, :]
        u[f, ny + 3 : ny + 5, :] = u[f, 3:5, :]
        u[f, ny + 5 : ny + 8, :] = rya[3 * f : 3 * f + 3, :]
    profiles, _ = primitives([u[f, ny : ny + SUBLANES, :] for f in range(5)])
    for f, difference in enumerate(flux_differences(profiles, up, down, 1)):
        df[f, ny : ny + SUBLANES, :] = difference

    for copy in halos[2:]:
        copy.wait_recv()
    total = ny + SUBLANES
    lane = lax.broadcasted_iota(jnp.int32, (total, LANES), 1)
    below = lax.broadcasted_iota(jnp.int32, (SUBLANES, LANES), 0) < 4
    far_left = jnp.concatenate([rxl[...], jnp.where(below, rc[2], rc[0])], axis=0)
    far_right = jnp.concatenate([rxr[...], jnp.where(below, rc[3], rc[1])], axis=0)
    seam = []
    for f in range(5):
        begin = u[f, :, 0:LANES]
        end = pltpu.roll(u[f, :, nx - LANES : nx], 64, 1)
        before = pltpu.roll(far_left, 125 - 8 * f, 1)
        after = pltpu.roll(far_right, 64 - 8 * f, 1)
        tile = jnp.where(lane < 32, begin, end)
        tile = jnp.where(lane >= 125, before, tile)
        seam.append(jnp.where((lane >= 64) & (lane < 67), after, tile))
    profiles, _ = primitives(seam)
    up, down = shifts(LANES, 1)
    for f, difference in enumerate(flux_differences(profiles, up, down, 1)):
        df[f, :, 0:LANES] = jnp.where(lane < 3, difference, df[f, :, 0:LANES])
        df[f, :, nx - LANES : nx] = jnp.where(
            lane >= 125, pltpu.roll(difference, 64, 1), df[f, :, nx - LANES : nx]
        )

    pltpu.make_async_copy(others, others, peak_recv).wait()
    peak = jnp.maximum(mine[...], jnp.max(others[...], axis=0))
    peak = jnp.max(peak, axis=1, keepdims=True)
    half_step = (0.5 * COURANT) / peak

    up, down = shifts(total, 0)
    for c in range(0, nx, LANES):
        cells = [
            u[f, :, c : c + LANES] - half_step * df[f, :, c : c + LANES] for f in range(5)
        ]
        profiles, _ = primitives(cells)
        for f, difference in enumerate(flux_differences(profiles, up, down, 2)):
            result = cells[f] - half_step * difference
            out[f, 0, :, c : c + LANES] = result[0:ny]

    for copy in halos:
        copy.wait_send()
    pltpu.make_async_copy(others, others, peak_send).wait()


def local(rows, cols, fields):
    ny, nx = fields.shape[2], fields.shape[3]
    vmem = lambda *shape: pltpu.VMEM(shape, jnp.float32)
    dma = pltpu.SemaphoreType.DMA
    return pl.pallas_call(
        functools.partial(kernel, rows, cols),
        out_shape=jax.ShapeDtypeStruct(fields.shape, fields.dtype),
        in_specs=[pl.BlockSpec(memory_space=pltpu.HBM)],
        out_specs=pl.BlockSpec(memory_space=pltpu.VMEM),
        scratch_shapes=[
            vmem(5, ny + SUBLANES, nx),
            vmem(5, ny + SUBLANES, nx),
            vmem(5, ny, nx),
            vmem(ny, LANES),
            vmem(ny, LANES),
            vmem(16, nx),
            vmem(16, nx),
            vmem(ny, LANES),
            vmem(ny, LANES),
            vmem(16, nx),
            vmem(16, nx),
            vmem(4, SUBLANES, LANES),
            vmem(1, LANES),
            vmem(rows * cols - 1, 1, LANES),
            dma,
            dma((8,)),
            dma((8,)),
            dma,
            dma,
        ],
        compiler_params=pltpu.CompilerParams(
            collective_id=0, has_side_effects=True, vmem_limit_bytes=32 * 1024 * 1024
        ),
        name="sweeps",
    )(fields)


def solution(mesh):
    spec = P(None, None, "col", "row")
    return jax.shard_map(
        functools.partial(local, mesh.shape["row"], mesh.shape["col"]),
        mesh=mesh,
        in_specs=(spec,),
        out_specs=spec,
        check_vma=False,
    )
```

```python
import functools

import jax
import jax.numpy as jnp
from jax import lax
from jax.experimental import pallas as pl
from jax.experimental.pallas import tpu as pltpu
from jax.sharding import PartitionSpec as P

GAMMA = 1.4
COURANT = 0.3
MESH = pl.DeviceIdType.MESH
LANES = 128
SUBLANES = 8
TINY = 1e-37
UNROLLED = 64


def inverse(value):
    guess = pl.reciprocal(value, approx=True)
    return guess * (2.0 - value * guess)


def root(value):
    return value * lax.rsqrt(jnp.maximum(value, TINY))


def primitives(cells):
    density = cells[0]
    inverse_density = inverse(density)
    velocity = [cells[k] * inverse_density for k in (1, 2, 3)]
    square = velocity[0] * velocity[0] + velocity[1] * velocity[1] + velocity[2] * velocity[2]
    pressure = (GAMMA - 1.0) * (cells[4] - 0.5 * density * square)
    return [density] + velocity + [pressure], inverse_density


def limited(first, second):
    return jnp.minimum(jnp.maximum(first, jnp.minimum(second, 0.0)), jnp.maximum(second, 0.0))


def face_values(q, up, down):
    after = up(q)
    edge = 7.0 / 12.0 * (q + after) - 1.0 / 12.0 * (down(q) + up(after))
    edge = jnp.minimum(jnp.maximum(edge, jnp.minimum(q, after)), jnp.maximum(q, after))
    rise = edge - q
    fall = q - down(edge)
    right = q + limited(rise, fall + fall)
    left = q - limited(fall, rise + rise)
    return right, up(left)


def face_terms(state, normal):
    density, pressure = state[0], state[4]
    velocity = state[1:4]
    square = velocity[0] * velocity[0] + velocity[1] * velocity[1] + velocity[2] * velocity[2]
    energy = pressure * (1.0 / (GAMMA - 1.0)) + 0.5 * density * square
    speed = velocity[normal - 1]
    momentum = [density * v for v in velocity]
    mass_flux = momentum[normal - 1]
    flux = [mass_flux] + [mass_flux * v for v in velocity] + [speed * (energy + pressure)]
    flux[normal] = flux[normal] + pressure
    signal = jnp.abs(speed) + root(GAMMA * pressure * inverse(density))
    return [density] + momentum + [energy], flux, signal


def flux_differences(profiles, up, down, normal):
    pairs = [face_values(q, up, down) for q in profiles]
    left_cons, left_flux, left_signal = face_terms([a for a, _ in pairs], normal)
    right_cons, right_flux, right_signal = face_terms([b for _, b in pairs], normal)
    signal = jnp.maximum(left_signal, right_signal)
    results = []
    for k in range(5):
        flux = (left_flux[k] + right_flux[k]) - signal * (right_cons[k] - left_cons[k])
        results.append(flux - down(flux))
    return results


def shifts(length, axis):
    return (
        lambda a: pltpu.roll(a, length - 1, axis),
        lambda a: pltpu.roll(a, 1, axis),
    )


def kernel(
    rows, cols, x, out, u, df, prim, xr, xl, yt, yb, rxl, rxr, rya, ryb, rc, mine, others,
    in_sem, halo_send, halo_recv, peak_send, peak_recv,
):
    ny, nx = x.shape[2], x.shape[3]
    me_r, me_c = lax.axis_index("row"), lax.axis_index("col")

    def row_at(step):
        return lax.rem(me_r + (step % rows), rows)

    def col_at(step):
        return lax.rem(me_c + (step % cols), cols)

    load = pltpu.make_async_copy(x.at[:, 0], u.at[:, pl.ds(0, ny)], in_sem)
    load.start()

    barrier = pltpu.get_barrier_semaphore()
    count = rows * cols

    def for_peers(act):
        if count <= UNROLLED:
            at_row = [row_at(a) for a in range(rows)]
            at_col = [col_at(b) for b in range(cols)]
            for d in range(1, count):
                act(d, (at_row[d // cols], at_col[d % cols]))
        else:

            @pl.loop(1, count)
            def _(d):
                act(d, (lax.rem(me_r + d // cols, rows), lax.rem(me_c + d % cols, cols)))

    def greet(d, peer):
        pl.semaphore_signal(barrier, inc=1, device_id=peer, device_id_type=MESH)

    for_peers(greet)

    load.wait()

    peak = None
    for r in range(0, ny, SUBLANES):
        profiles, inverse_density = primitives([u[f, r : r + SUBLANES, :] for f in range(5)])
        for f in range(5):
            prim[f, r : r + SUBLANES, :] = profiles[f]
        speed = jnp.maximum(jnp.abs(profiles[1]), jnp.abs(profiles[2]))
        speed = speed + root(GAMMA * profiles[4] * inverse_density)
        for c in range(0, nx, LANES):
            part = speed[:, c : c + LANES]
            peak = part if peak is None else jnp.maximum(peak, part)
    mine[...] = jnp.max(peak, axis=0, keepdims=True)

    lane = lax.broadcasted_iota(jnp.int32, (ny, LANES), 1)
    pack_r = pack_l = None
    for f in range(5):
        edge_r = pltpu.roll(u[f, 0:ny, nx - LANES : nx], 8 * f + 3, 1)
        edge_l = u[f, 0:ny, 0:LANES]
        if f:
            edge_l = pltpu.roll(edge_l, 8 * f, 1)
            pack_r = jnp.where(lane < 8 * f, pack_r, edge_r)
            pack_l = jnp.where(lane < 8 * f, pack_l, edge_l)
        else:
            pack_r, pack_l = edge_r, edge_l
    xr[...] = pack_r
    xl[...] = pack_l
    for f in range(5):
        yt[3 * f : 3 * f + 3, :] = u[f, 0:3, :]
        yb[3 * f : 3 * f + 3, :] = u[f, ny - 3 : ny, :]
    yt[15:16, :] = u[0, 0:1, :]
    yb[15:16, :] = u[0, 0:1, :]
    pl.semaphore_wait(barrier, count - 1)
    top, bottom = pl.ds(0, SUBLANES), pl.ds(ny - SUBLANES, SUBLANES)
    halos = []
    for i, (src, dst, device) in enumerate(
        [
            (yb, rya, (me_r, col_at(1))),
            (yt, ryb, (me_r, col_at(-1))),
            (xr, rxl, (row_at(1), me_c)),
            (xl, rxr, (row_at(-1), me_c)),
            (xr.at[bottom], rc.at[0], (row_at(1), col_at(1))),
            (xl.at[bottom], rc.at[1], (row_at(-1), col_at(1))),
            (xr.at[top], rc.at[2], (row_at(1), col_at(-1))),
            (xl.at[top], rc.at[3], (row_at(-1), col_at(-1))),
        ]
    ):
        halos.append(
            pltpu.make_async_remote_copy(
                src_ref=src, dst_ref=dst, send_sem=halo_send.at[i], recv_sem=halo_recv.at[i],
                device_id=device, device_id_type=MESH,
            )
        )
        halos[i].start()

    def tell(d, peer):
        pltpu.make_async_remote_copy(
            src_ref=mine, dst_ref=others.at[d - 1], send_sem=peak_send, recv_sem=peak_recv,
            device_id=peer, device_id_type=MESH,
        ).start()

    for_peers(tell)

    up, down = shifts(nx, 1)
    for r in range(0, ny, SUBLANES):
        profiles = [prim[f, r : r + SUBLANES, :] for f in range(5)]
        for f, difference in enumerate(flux_differences(profiles, up, down, 1)):
            df[f, r : r + SUBLANES, :] = difference

    halos[0].wait_recv()
    halos[1].wait_recv()
    for f in range(5):
        u[f, ny : ny + 3, :] = ryb[3 * f : 3 * f + 3, :]
        u[f, ny + 3 : ny + 5, :] = u[f, 3:5, :]
        u[f, ny + 5 : ny + 8, :] = rya[3 * f : 3 * f + 3, :]
    profiles, _ = primitives([u[f, ny : ny + SUBLANES, :] for f in range(5)])
    for f, difference in enumerate(flux_differences(profiles, up, down, 1)):
        df[f, ny : ny + SUBLANES, :] = difference

    for copy in halos[2:]:
        copy.wait_recv()
    total = ny + SUBLANES
    lane = lax.broadcasted_iota(jnp.int32, (total, LANES), 1)
    below = lax.broadcasted_iota(jnp.int32, (SUBLANES, LANES), 0) < 4
    far_left = jnp.concatenate([rxl[...], jnp.where(below, rc[2], rc[0])], axis=0)
    far_right = jnp.concatenate([rxr[...], jnp.where(below, rc[3], rc[1])], axis=0)
    seam = []
    for f in range(5):
        begin = u[f, :, 0:LANES]
        end = pltpu.roll(u[f, :, nx - LANES : nx], 64, 1)
        before = pltpu.roll(far_left, 125 - 8 * f, 1)
        after = pltpu.roll(far_right, 64 - 8 * f, 1)
        tile = jnp.where(lane < 32, begin, end)
        tile = jnp.where(lane >= 125, before, tile)
        seam.append(jnp.where((lane >= 64) & (lane < 67), after, tile))
    profiles, _ = primitives(seam)
    up, down = shifts(LANES, 1)
    for f, difference in enumerate(flux_differences(profiles, up, down, 1)):
        df[f, :, 0:LANES] = jnp.where(lane < 3, difference, df[f, :, 0:LANES])
        df[f, :, nx - LANES : nx] = jnp.where(
            lane >= 125, pltpu.roll(difference, 64, 1), df[f, :, nx - LANES : nx]
        )

    pltpu.make_async_copy(others, others, peak_recv).wait()
    peak = jnp.maximum(mine[...], jnp.max(others[...], axis=0))
    peak = jnp.max(peak, axis=1, keepdims=True)
    half_step = (0.5 * COURANT) / peak

    up, down = shifts(total, 0)
    for c in range(0, nx, LANES):
        cells = [
            u[f, :, c : c + LANES] - half_step * df[f, :, c : c + LANES] for f in range(5)
        ]
        profiles, _ = primitives(cells)
        for f, difference in enumerate(flux_differences(profiles, up, down, 2)):
            result = cells[f] - half_step * difference
            out[f, 0, :, c : c + LANES] = result[0:ny]

    for copy in halos:
        copy.wait_send()
    pltpu.make_async_copy(others, others, peak_send).wait()


def local(rows, cols, fields):
    ny, nx = fields.shape[2], fields.shape[3]
    vmem = lambda *shape: pltpu.VMEM(shape, jnp.float32)
    dma = pltpu.SemaphoreType.DMA
    return pl.pallas_call(
        functools.partial(kernel, rows, cols),
        out_shape=jax.ShapeDtypeStruct(fields.shape, fields.dtype),
        in_specs=[pl.BlockSpec(memory_space=pltpu.HBM)],
        out_specs=pl.BlockSpec(memory_space=pltpu.VMEM),
        scratch_shapes=[
            vmem(5, ny + SUBLANES, nx),
            vmem(5, ny + SUBLANES, nx),
            vmem(5, ny, nx),
            vmem(ny, LANES),
            vmem(ny, LANES),
            vmem(16, nx),
            vmem(16, nx),
            vmem(ny, LANES),
            vmem(ny, LANES),
            vmem(16, nx),
            vmem(16, nx),
            vmem(4, SUBLANES, LANES),
            vmem(1, LANES),
            vmem(rows * cols - 1, 1, LANES),
            dma,
            dma((8,)),
            dma((8,)),
            dma,
            dma,
        ],
        compiler_params=pltpu.CompilerParams(
            collective_id=0, has_side_effects=True, vmem_limit_bytes=55072 * 1024
        ),
        name="sweeps",
    )(fields)


def solution(mesh):
    spec = P(None, None, "col", "row")
    return jax.shard_map(
        functools.partial(local, mesh.shape["row"], mesh.shape["col"]),
        mesh=mesh,
        in_specs=(spec,),
        out_specs=spec,
        check_vma=False,
    )
```

```python
import functools

import jax
import jax.numpy as jnp
from jax import lax
from jax.experimental import pallas as pl
from jax.experimental.pallas import tpu as pltpu
from jax.sharding import PartitionSpec as P

GAMMA = 1.4
COURANT = 0.3
MESH = pl.DeviceIdType.MESH
LANES = 128
SUBLANES = 8
TINY = 1e-37
UNROLLED = 64


def inverse(value):
    guess = pl.reciprocal(value, approx=True)
    return guess * (2.0 - value * guess)


def root(value):
    return value * lax.rsqrt(jnp.maximum(value, TINY))


def primitives(cells):
    density = cells[0]
    inverse_density = inverse(density)
    velocity = [cells[k] * inverse_density for k in (1, 2, 3)]
    square = velocity[0] * velocity[0] + velocity[1] * velocity[1] + velocity[2] * velocity[2]
    pressure = (GAMMA - 1.0) * (cells[4] - 0.5 * density * square)
    return [density] + velocity + [pressure], inverse_density


def limited(first, second):
    return jnp.minimum(jnp.maximum(first, jnp.minimum(second, 0.0)), jnp.maximum(second, 0.0))


def face_values(q, up, down):
    after = up(q)
    jump = after - q
    rise = 0.5 * jump + (1.0 / 12.0) * (down(jump) - up(jump))
    rise = jnp.minimum(jnp.maximum(rise, jnp.minimum(jump, 0.0)), jnp.maximum(jump, 0.0))
    next_fall = jump - rise
    fall, next_rise = down(next_fall), up(rise)
    right = q + limited(rise, fall + fall)
    next_left = after - limited(next_fall, next_rise + next_rise)
    return right, next_left


def face_terms(state, normal):
    density, pressure = state[0], state[4]
    velocity = state[1:4]
    momentum = [density * v for v in velocity]
    square = momentum[0] * velocity[0] + momentum[1] * velocity[1] + momentum[2] * velocity[2]
    energy = pressure * (1.0 / (GAMMA - 1.0)) + 0.5 * square
    speed = velocity[normal - 1]
    mass_flux = momentum[normal - 1]
    flux = [mass_flux] + [mass_flux * v for v in velocity] + [speed * (energy + pressure)]
    flux[normal] = flux[normal] + pressure
    signal = jnp.abs(speed) + root(GAMMA * pressure * inverse(density))
    return [density] + momentum + [energy], flux, signal


def flux_differences(profiles, up, down, normal):
    pairs = [face_values(q, up, down) for q in profiles]
    left_cons, left_flux, left_signal = face_terms([a for a, _ in pairs], normal)
    right_cons, right_flux, right_signal = face_terms([b for _, b in pairs], normal)
    signal = jnp.maximum(left_signal, right_signal)
    results = []
    for k in range(5):
        flux = (left_flux[k] + right_flux[k]) - signal * (right_cons[k] - left_cons[k])
        results.append(flux - down(flux))
    return results


def shifts(length, axis):
    return (
        lambda a: pltpu.roll(a, length - 1, axis),
        lambda a: pltpu.roll(a, 1, axis),
    )


def kernel(
    rows, cols, x, out, u, df, prim, xr, xl, yt, yb, rxl, rxr, rya, ryb, rc, mine, others,
    in_sem, halo_send, halo_recv, peak_send, peak_recv,
):
    ny, nx = x.shape[2], x.shape[3]
    me_r, me_c = lax.axis_index("row"), lax.axis_index("col")

    def row_at(step):
        return lax.rem(me_r + (step % rows), rows)

    def col_at(step):
        return lax.rem(me_c + (step % cols), cols)

    load = pltpu.make_async_copy(x.at[:, 0], u.at[:, pl.ds(0, ny)], in_sem)
    load.start()

    barrier = pltpu.get_barrier_semaphore()
    count = rows * cols

    def for_peers(act):
        if count <= UNROLLED:
            at_row = [row_at(a) for a in range(rows)]
            at_col = [col_at(b) for b in range(cols)]
            for d in range(1, count):
                act(d, (at_row[d // cols], at_col[d % cols]))
        else:

            @pl.loop(1, count)
            def _(d):
                act(d, (lax.rem(me_r + d // cols, rows), lax.rem(me_c + d % cols, cols)))

    def greet(d, peer):
        pl.semaphore_signal(barrier, inc=1, device_id=peer, device_id_type=MESH)

    for_peers(greet)

    load.wait()

    peak = None
    for r in range(0, ny, SUBLANES):
        profiles, inverse_density = primitives([u[f, r : r + SUBLANES, :] for f in range(5)])
        for f in range(5):
            prim[f, r : r + SUBLANES, :] = profiles[f]
        speed = jnp.maximum(jnp.abs(profiles[1]), jnp.abs(profiles[2]))
        speed = speed + root(GAMMA * profiles[4] * inverse_density)
        for c in range(0, nx, LANES):
            part = speed[:, c : c + LANES]
            peak = part if peak is None else jnp.maximum(peak, part)
    mine[...] = jnp.max(peak, axis=0, keepdims=True)

    lane = lax.broadcasted_iota(jnp.int32, (ny, LANES), 1)
    pack_r = pack_l = None
    for f in range(5):
        edge_r = pltpu.roll(u[f, 0:ny, nx - LANES : nx], 8 * f + 3, 1)
        edge_l = u[f, 0:ny, 0:LANES]
        if f:
            edge_l = pltpu.roll(edge_l, 8 * f, 1)
            pack_r = jnp.where(lane < 8 * f, pack_r, edge_r)
            pack_l = jnp.where(lane < 8 * f, pack_l, edge_l)
        else:
            pack_r, pack_l = edge_r, edge_l
    xr[...] = pack_r
    xl[...] = pack_l
    for f in range(5):
        yt[3 * f : 3 * f + 3, :] = u[f, 0:3, :]
        yb[3 * f : 3 * f + 3, :] = u[f, ny - 3 : ny, :]
    yt[15:16, :] = u[0, 0:1, :]
    yb[15:16, :] = u[0, 0:1, :]
    pl.semaphore_wait(barrier, count - 1)
    top, bottom = pl.ds(0, SUBLANES), pl.ds(ny - SUBLANES, SUBLANES)
    halos = []
    for i, (src, dst, device) in enumerate(
        [
            (yb, rya, (me_r, col_at(1))),
            (yt, ryb, (me_r, col_at(-1))),
            (xr, rxl, (row_at(1), me_c)),
            (xl, rxr, (row_at(-1), me_c)),
            (xr.at[bottom], rc.at[0], (row_at(1), col_at(1))),
            (xl.at[bottom], rc.at[1], (row_at(-1), col_at(1))),
            (xr.at[top], rc.at[2], (row_at(1), col_at(-1))),
            (xl.at[top], rc.at[3], (row_at(-1), col_at(-1))),
        ]
    ):
        halos.append(
            pltpu.make_async_remote_copy(
                src_ref=src, dst_ref=dst, send_sem=halo_send.at[i], recv_sem=halo_recv.at[i],
                device_id=device, device_id_type=MESH,
            )
        )
        halos[i].start()

    def tell(d, peer):
        pltpu.make_async_remote_copy(
            src_ref=mine, dst_ref=others.at[d - 1], send_sem=peak_send, recv_sem=peak_recv,
            device_id=peer, device_id_type=MESH,
        ).start()

    for_peers(tell)

    up, down = shifts(nx, 1)
    for r in range(0, ny, SUBLANES):
        profiles = [prim[f, r : r + SUBLANES, :] for f in range(5)]
        for f, difference in enumerate(flux_differences(profiles, up, down, 1)):
            df[f, r : r + SUBLANES, :] = difference

    halos[0].wait_recv()
    halos[1].wait_recv()
    for f in range(5):
        u[f, ny : ny + 3, :] = ryb[3 * f : 3 * f + 3, :]
        u[f, ny + 3 : ny + 5, :] = u[f, 3:5, :]
        u[f, ny + 5 : ny + 8, :] = rya[3 * f : 3 * f + 3, :]
    profiles, _ = primitives([u[f, ny : ny + SUBLANES, :] for f in range(5)])
    for f, difference in enumerate(flux_differences(profiles, up, down, 1)):
        df[f, ny : ny + SUBLANES, :] = difference

    for copy in halos[2:]:
        copy.wait_recv()
    total = ny + SUBLANES
    lane = lax.broadcasted_iota(jnp.int32, (total, LANES), 1)
    below = lax.broadcasted_iota(jnp.int32, (SUBLANES, LANES), 0) < 4
    far_left = jnp.concatenate([rxl[...], jnp.where(below, rc[2], rc[0])], axis=0)
    far_right = jnp.concatenate([rxr[...], jnp.where(below, rc[3], rc[1])], axis=0)
    seam = []
    for f in range(5):
        begin = u[f, :, 0:LANES]
        end = pltpu.roll(u[f, :, nx - LANES : nx], 64, 1)
        before = pltpu.roll(far_left, 125 - 8 * f, 1)
        after = pltpu.roll(far_right, 64 - 8 * f, 1)
        tile = jnp.where(lane < 32, begin, end)
        tile = jnp.where(lane >= 125, before, tile)
        seam.append(jnp.where((lane >= 64) & (lane < 67), after, tile))
    profiles, _ = primitives(seam)
    up, down = shifts(LANES, 1)
    for f, difference in enumerate(flux_differences(profiles, up, down, 1)):
        df[f, :, 0:LANES] = jnp.where(lane < 3, difference, df[f, :, 0:LANES])
        df[f, :, nx - LANES : nx] = jnp.where(
            lane >= 125, pltpu.roll(difference, 64, 1), df[f, :, nx - LANES : nx]
        )

    pltpu.make_async_copy(others, others, peak_recv).wait()
    peak = jnp.maximum(mine[...], jnp.max(others[...], axis=0))
    peak = jnp.max(peak, axis=1, keepdims=True)
    half_step = (0.5 * COURANT) / peak

    up, down = shifts(total, 0)
    for c in range(0, nx, LANES):
        cells = [
            u[f, :, c : c + LANES] - half_step * df[f, :, c : c + LANES] for f in range(5)
        ]
        profiles, _ = primitives(cells)
        for f, difference in enumerate(flux_differences(profiles, up, down, 2)):
            result = cells[f] - half_step * difference
            out[f, 0, :, c : c + LANES] = result[0:ny]

    for copy in halos:
        copy.wait_send()
    pltpu.make_async_copy(others, others, peak_send).wait()


def local(rows, cols, fields):
    ny, nx = fields.shape[2], fields.shape[3]
    vmem = lambda *shape: pltpu.VMEM(shape, jnp.float32)
    dma = pltpu.SemaphoreType.DMA
    return pl.pallas_call(
        functools.partial(kernel, rows, cols),
        out_shape=jax.ShapeDtypeStruct(fields.shape, fields.dtype),
        in_specs=[pl.BlockSpec(memory_space=pltpu.HBM)],
        out_specs=pl.BlockSpec(memory_space=pltpu.VMEM),
        scratch_shapes=[
            vmem(5, ny + SUBLANES, nx),
            vmem(5, ny + SUBLANES, nx),
            vmem(5, ny, nx),
            vmem(ny, LANES),
            vmem(ny, LANES),
            vmem(16, nx),
            vmem(16, nx),
            vmem(ny, LANES),
            vmem(ny, LANES),
            vmem(16, nx),
            vmem(16, nx),
            vmem(4, SUBLANES, LANES),
            vmem(1, LANES),
            vmem(rows * cols - 1, 1, LANES),
            dma,
            dma((8,)),
            dma((8,)),
            dma,
            dma,
        ],
        compiler_params=pltpu.CompilerParams(
            collective_id=0, has_side_effects=True, vmem_limit_bytes=55072 * 1024
        ),
        name="sweeps",
    )(fields)


def solution(mesh):
    spec = P(None, None, "col", "row")
    return jax.shard_map(
        functools.partial(local, mesh.shape["row"], mesh.shape["col"]),
        mesh=mesh,
        in_specs=(spec,),
        out_specs=spec,
        check_vma=False,
    )
```

```python
import functools

import jax
import jax.numpy as jnp
from jax import lax
from jax.experimental import pallas as pl
from jax.experimental.pallas import tpu as pltpu
from jax.sharding import PartitionSpec as P

GAMMA = 1.4
COURANT = 0.3
MESH = pl.DeviceIdType.MESH
LANES = 128
SUBLANES = 8
TINY = 1e-37
UNROLLED = 64


def inverse(value):
    guess = pl.reciprocal(value, approx=True)
    return guess * (2.0 - value * guess)


def root(value):
    return value * lax.rsqrt(jnp.maximum(value, TINY))


def primitives(cells):
    density = cells[0]
    inverse_density = inverse(density)
    velocity = [cells[k] * inverse_density for k in (1, 2, 3)]
    square = velocity[0] * velocity[0] + velocity[1] * velocity[1] + velocity[2] * velocity[2]
    pressure = (GAMMA - 1.0) * (cells[4] - 0.5 * density * square)
    return [density] + velocity + [pressure], inverse_density


def limited(first, second):
    return jnp.minimum(jnp.maximum(first, jnp.minimum(second, 0.0)), jnp.maximum(second, 0.0))


def face_values(q, up, down):
    after = up(q)
    jump = after - q
    rise = 0.5 * jump + (1.0 / 12.0) * (down(jump) - up(jump))
    rise = jnp.minimum(jnp.maximum(rise, jnp.minimum(jump, 0.0)), jnp.maximum(jump, 0.0))
    next_fall = jump - rise
    fall, next_rise = down(next_fall), up(rise)
    right = q + limited(rise, fall + fall)
    next_left = after - limited(next_fall, next_rise + next_rise)
    return right, next_left


def face_terms(state, normal):
    density, pressure = state[0], state[4]
    velocity = state[1:4]
    momentum = [density * v for v in velocity]
    square = momentum[0] * velocity[0] + momentum[1] * velocity[1] + momentum[2] * velocity[2]
    energy = pressure * (1.0 / (GAMMA - 1.0)) + 0.5 * square
    speed = velocity[normal - 1]
    mass_flux = momentum[normal - 1]
    flux = [mass_flux] + [mass_flux * v for v in velocity] + [speed * (energy + pressure)]
    flux[normal] = flux[normal] + pressure
    signal = jnp.abs(speed) + root(GAMMA * pressure * inverse(density))
    return [density] + momentum + [energy], flux, signal


def flux_differences(profiles, up, down, normal):
    pairs = [face_values(q, up, down) for q in profiles]
    left_cons, left_flux, left_signal = face_terms([a for a, _ in pairs], normal)
    right_cons, right_flux, right_signal = face_terms([b for _, b in pairs], normal)
    signal = jnp.maximum(left_signal, right_signal)
    results = []
    for k in range(5):
        flux = (left_flux[k] + right_flux[k]) - signal * (right_cons[k] - left_cons[k])
        results.append(flux - down(flux))
    return results


def shifts(length, axis):
    return (
        lambda a: pltpu.roll(a, length - 1, axis),
        lambda a: pltpu.roll(a, 1, axis),
    )


def kernel(
    rows, cols, x, out, u, df, xr, xl, yt, yb, rxl, rxr, rya, ryb, rc, mine, others,
    in_sem, halo_send, halo_recv, peak_send, peak_recv,
):
    ny, nx = x.shape[2], x.shape[3]
    me_r, me_c = lax.axis_index("row"), lax.axis_index("col")

    def row_at(step):
        return lax.rem(me_r + (step % rows), rows)

    def col_at(step):
        return lax.rem(me_c + (step % cols), cols)

    load = pltpu.make_async_copy(x.at[:, 0], u.at[:, pl.ds(0, ny)], in_sem)
    load.start()

    barrier = pltpu.get_barrier_semaphore()
    count = rows * cols

    def for_peers(act):
        if count <= UNROLLED:
            at_row = [row_at(a) for a in range(rows)]
            at_col = [col_at(b) for b in range(cols)]
            for d in range(1, count):
                act(d, (at_row[d // cols], at_col[d % cols]))
        else:

            @pl.loop(1, count)
            def _(d):
                act(d, (lax.rem(me_r + d // cols, rows), lax.rem(me_c + d % cols, cols)))

    def greet(d, peer):
        pl.semaphore_signal(barrier, inc=1, device_id=peer, device_id_type=MESH)

    for_peers(greet)

    load.wait()

    peak = None
    for r in range(0, ny, SUBLANES):
        profiles, inverse_density = primitives([u[f, r : r + SUBLANES, :] for f in range(5)])
        speed = jnp.maximum(jnp.abs(profiles[1]), jnp.abs(profiles[2]))
        speed = speed + root(GAMMA * profiles[4] * inverse_density)
        for c in range(0, nx, LANES):
            part = speed[:, c : c + LANES]
            peak = part if peak is None else jnp.maximum(peak, part)
    mine[...] = jnp.max(peak, axis=0, keepdims=True)

    lane = lax.broadcasted_iota(jnp.int32, (ny, LANES), 1)
    pack_r = pack_l = None
    for f in range(5):
        edge_r = pltpu.roll(u[f, 0:ny, nx - LANES : nx], 8 * f + 3, 1)
        edge_l = u[f, 0:ny, 0:LANES]
        if f:
            edge_l = pltpu.roll(edge_l, 8 * f, 1)
            pack_r = jnp.where(lane < 8 * f, pack_r, edge_r)
            pack_l = jnp.where(lane < 8 * f, pack_l, edge_l)
        else:
            pack_r, pack_l = edge_r, edge_l
    xr[...] = pack_r
    xl[...] = pack_l
    for f in range(5):
        yt[3 * f : 3 * f + 3, :] = u[f, 0:3, :]
        yb[3 * f : 3 * f + 3, :] = u[f, ny - 3 : ny, :]
    yt[15:16, :] = u[0, 0:1, :]
    yb[15:16, :] = u[0, 0:1, :]
    pl.semaphore_wait(barrier, count - 1)
    top, bottom = pl.ds(0, SUBLANES), pl.ds(ny - SUBLANES, SUBLANES)
    halos = []
    for i, (src, dst, device) in enumerate(
        [
            (yb, rya, (me_r, col_at(1))),
            (yt, ryb, (me_r, col_at(-1))),
            (xr, rxl, (row_at(1), me_c)),
            (xl, rxr, (row_at(-1), me_c)),
            (xr.at[bottom], rc.at[0], (row_at(1), col_at(1))),
            (xl.at[bottom], rc.at[1], (row_at(-1), col_at(1))),
            (xr.at[top], rc.at[2], (row_at(1), col_at(-1))),
            (xl.at[top], rc.at[3], (row_at(-1), col_at(-1))),
        ]
    ):
        halos.append(
            pltpu.make_async_remote_copy(
                src_ref=src, dst_ref=dst, send_sem=halo_send.at[i], recv_sem=halo_recv.at[i],
                device_id=device, device_id_type=MESH,
            )
        )
        halos[i].start()

    def tell(d, peer):
        pltpu.make_async_remote_copy(
            src_ref=mine, dst_ref=others.at[d - 1], send_sem=peak_send, recv_sem=peak_recv,
            device_id=peer, device_id_type=MESH,
        ).start()

    for_peers(tell)

    up, down = shifts(nx, 1)

    @pl.loop(0, ny // SUBLANES + 1)
    def _(tile):
        @pl.when(tile == ny // SUBLANES)
        def _():
            halos[0].wait_recv()
            halos[1].wait_recv()
            for f in range(5):
                u[f, ny : ny + 3, :] = ryb[3 * f : 3 * f + 3, :]
                u[f, ny + 3 : ny + 5, :] = u[f, 3:5, :]
                u[f, ny + 5 : ny + 8, :] = rya[3 * f : 3 * f + 3, :]

        at = pl.ds(pl.multiple_of(tile * SUBLANES, SUBLANES), SUBLANES)
        profiles, _ = primitives([u[f, at, :] for f in range(5)])
        for f, difference in enumerate(flux_differences(profiles, up, down, 1)):
            df[f, at, :] = difference

    for copy in halos[2:]:
        copy.wait_recv()
    total = ny + SUBLANES
    lane = lax.broadcasted_iota(jnp.int32, (total, LANES), 1)
    below = lax.broadcasted_iota(jnp.int32, (SUBLANES, LANES), 0) < 4
    far_left = jnp.concatenate([rxl[...], jnp.where(below, rc[2], rc[0])], axis=0)
    far_right = jnp.concatenate([rxr[...], jnp.where(below, rc[3], rc[1])], axis=0)
    seam = []
    for f in range(5):
        begin = u[f, :, 0:LANES]
        end = pltpu.roll(u[f, :, nx - LANES : nx], 64, 1)
        before = pltpu.roll(far_left, 125 - 8 * f, 1)
        after = pltpu.roll(far_right, 64 - 8 * f, 1)
        tile = jnp.where(lane < 32, begin, end)
        tile = jnp.where(lane >= 125, before, tile)
        seam.append(jnp.where((lane >= 64) & (lane < 67), after, tile))
    profiles, _ = primitives(seam)
    up, down = shifts(LANES, 1)
    for f, difference in enumerate(flux_differences(profiles, up, down, 1)):
        df[f, :, 0:LANES] = jnp.where(lane < 3, difference, df[f, :, 0:LANES])
        df[f, :, nx - LANES : nx] = jnp.where(
            lane >= 125, pltpu.roll(difference, 64, 1), df[f, :, nx - LANES : nx]
        )

    pltpu.make_async_copy(others, others, peak_recv).wait()
    peak = jnp.maximum(mine[...], jnp.max(others[...], axis=0))
    peak = jnp.max(peak, axis=1, keepdims=True)
    half_step = (0.5 * COURANT) / peak

    up, down = shifts(total, 0)

    @pl.loop(0, nx // LANES)
    def _(chunk):
        at = pl.ds(pl.multiple_of(chunk * LANES, LANES), LANES)
        cells = [u[f, :, at] - half_step * df[f, :, at] for f in range(5)]
        profiles, _ = primitives(cells)
        for f, difference in enumerate(flux_differences(profiles, up, down, 2)):
            result = cells[f] - half_step * difference
            out[f, 0, :, at] = result[0:ny]

    for copy in halos:
        copy.wait_send()
    pltpu.make_async_copy(others, others, peak_send).wait()


def local(rows, cols, fields):
    ny, nx = fields.shape[2], fields.shape[3]
    vmem = lambda *shape: pltpu.VMEM(shape, jnp.float32)
    dma = pltpu.SemaphoreType.DMA
    return pl.pallas_call(
        functools.partial(kernel, rows, cols),
        out_shape=jax.ShapeDtypeStruct(fields.shape, fields.dtype),
        in_specs=[pl.BlockSpec(memory_space=pltpu.HBM)],
        out_specs=pl.BlockSpec(memory_space=pltpu.VMEM),
        scratch_shapes=[
            vmem(5, ny + SUBLANES, nx),
            vmem(5, ny + SUBLANES, nx),
            vmem(ny, LANES),
            vmem(ny, LANES),
            vmem(16, nx),
            vmem(16, nx),
            vmem(ny, LANES),
            vmem(ny, LANES),
            vmem(16, nx),
            vmem(16, nx),
            vmem(4, SUBLANES, LANES),
            vmem(1, LANES),
            vmem(rows * cols - 1, 1, LANES),
            dma,
            dma((8,)),
            dma((8,)),
            dma,
            dma,
        ],
        compiler_params=pltpu.CompilerParams(
            collective_id=0, has_side_effects=True, vmem_limit_bytes=55072 * 1024
        ),
        name="sweeps",
    )(fields)


def solution(mesh):
    spec = P(None, None, "col", "row")
    return jax.shard_map(
        functools.partial(local, mesh.shape["row"], mesh.shape["col"]),
        mesh=mesh,
        in_specs=(spec,),
        out_specs=spec,
        check_vma=False,
    )
```

```python
import functools

import jax
import jax.numpy as jnp
from jax import lax
from jax.experimental import pallas as pl
from jax.experimental.pallas import tpu as pltpu
from jax.sharding import PartitionSpec as P

GAMMA = 1.4
COURANT = 0.3
MESH = pl.DeviceIdType.MESH
LANES = 128
SUBLANES = 8
TINY = 1e-37
UNROLLED = 64


def inverse(value):
    guess = pl.reciprocal(value, approx=True)
    return guess * (2.0 - value * guess)


def root(value):
    return value * lax.rsqrt(jnp.maximum(value, TINY))


def primitives(cells):
    density = cells[0]
    inverse_density = inverse(density)
    velocity = [cells[k] * inverse_density for k in (1, 2, 3)]
    square = velocity[0] * velocity[0] + velocity[1] * velocity[1] + velocity[2] * velocity[2]
    pressure = (GAMMA - 1.0) * (cells[4] - 0.5 * density * square)
    return [density] + velocity + [pressure], inverse_density


def limited(first, second):
    return jnp.minimum(jnp.maximum(first, jnp.minimum(second, 0.0)), jnp.maximum(second, 0.0))


def face_values(q, up, down):
    after = up(q)
    jump = after - q
    rise = 0.5 * jump + (1.0 / 12.0) * (down(jump) - up(jump))
    rise = jnp.minimum(jnp.maximum(rise, jnp.minimum(jump, 0.0)), jnp.maximum(jump, 0.0))
    next_fall = jump - rise
    fall, next_rise = down(next_fall), up(rise)
    right = q + limited(rise, fall + fall)
    next_left = after - limited(next_fall, next_rise + next_rise)
    return right, next_left


def face_terms(state, normal):
    density, pressure = state[0], state[4]
    velocity = state[1:4]
    momentum = [density * v for v in velocity]
    square = momentum[0] * velocity[0] + momentum[1] * velocity[1] + momentum[2] * velocity[2]
    energy = pressure * (1.0 / (GAMMA - 1.0)) + 0.5 * square
    speed = velocity[normal - 1]
    mass_flux = momentum[normal - 1]
    flux = [mass_flux] + [mass_flux * v for v in velocity] + [speed * (energy + pressure)]
    flux[normal] = flux[normal] + pressure
    signal = jnp.abs(speed) + root(GAMMA * pressure * inverse(density))
    return [density] + momentum + [energy], flux, signal


def flux_differences(profiles, up, down, normal):
    pairs = [face_values(q, up, down) for q in profiles]
    left_cons, left_flux, left_signal = face_terms([a for a, _ in pairs], normal)
    right_cons, right_flux, right_signal = face_terms([b for _, b in pairs], normal)
    signal = jnp.maximum(left_signal, right_signal)
    results = []
    for k in range(5):
        flux = (left_flux[k] + right_flux[k]) - signal * (right_cons[k] - left_cons[k])
        results.append(flux - down(flux))
    return results


def shifts(length, axis):
    return (
        lambda a: pltpu.roll(a, length - 1, axis),
        lambda a: pltpu.roll(a, 1, axis),
    )


def kernel(
    rows, cols, x, out, u, df, xr, xl, yt, yb, rxl, rxr, rya, ryb, rc, mine, theirs, both, others,
    in_sem, halo_send, halo_recv, pair_send, pair_recv, peak_send, peak_recv,
):
    ny, nx = x.shape[2], x.shape[3]
    me_r, me_c = lax.axis_index("row"), lax.axis_index("col")

    def row_at(step):
        return lax.rem(me_r + (step % rows), rows)

    def col_at(step):
        return lax.rem(me_c + (step % cols), cols)

    load = pltpu.make_async_copy(x.at[:, 0], u.at[:, pl.ds(0, ny)], in_sem)
    load.start()

    barrier = pltpu.get_barrier_semaphore()
    partner = (me_r, me_c + 1 - 2 * lax.rem(me_c, 2))
    half = cols // 2
    count = rows * half

    def for_chips(act):
        if count <= UNROLLED:
            at_row = [row_at(a) for a in range(rows)]
            at_col = [col_at(2 * b) for b in range(half)]
            for d in range(1, count):
                act(d, (at_row[d // half], at_col[d % half]))
        else:

            @pl.loop(1, count)
            def _(d):
                step = 2 * (d % half)
                act(d, (lax.rem(me_r + d // half, rows), lax.rem(me_c + step, cols)))

    def greet(d, peer):
        pl.semaphore_signal(barrier, inc=1, device_id=peer, device_id_type=MESH)

    near = [(me_r, col_at(b)) for b in (1, -1)]
    near += [(row_at(a), col_at(b)) for a in (1, -1) for b in (1, -1)]
    for peer in near:
        greet(0, peer)
    for_chips(greet)
    load.wait()

    peak = None
    for r in range(0, ny, SUBLANES):
        profiles, inverse_density = primitives([u[f, r : r + SUBLANES, :] for f in range(5)])
        speed = jnp.maximum(jnp.abs(profiles[1]), jnp.abs(profiles[2]))
        speed = speed + root(GAMMA * profiles[4] * inverse_density)
        for c in range(0, nx, LANES):
            part = speed[:, c : c + LANES]
            peak = part if peak is None else jnp.maximum(peak, part)
    mine[...] = jnp.max(peak, axis=0, keepdims=True)

    lane = lax.broadcasted_iota(jnp.int32, (ny, LANES), 1)
    pack_r = pack_l = None
    for f in range(5):
        edge_r = pltpu.roll(u[f, 0:ny, nx - LANES : nx], 8 * f + 3, 1)
        edge_l = u[f, 0:ny, 0:LANES]
        if f:
            edge_l = pltpu.roll(edge_l, 8 * f, 1)
            pack_r = jnp.where(lane < 8 * f, pack_r, edge_r)
            pack_l = jnp.where(lane < 8 * f, pack_l, edge_l)
        else:
            pack_r, pack_l = edge_r, edge_l
    xr[...] = pack_r
    xl[...] = pack_l
    for f in range(5):
        yt[3 * f : 3 * f + 3, :] = u[f, 0:3, :]
        yb[3 * f : 3 * f + 3, :] = u[f, ny - 3 : ny, :]
    yt[15:16, :] = u[0, 0:1, :]
    yb[15:16, :] = u[0, 0:1, :]
    pl.semaphore_wait(barrier, count - 1 + len(near))
    pair = pltpu.make_async_remote_copy(
        src_ref=mine, dst_ref=theirs, send_sem=pair_send, recv_sem=pair_recv,
        device_id=partner, device_id_type=MESH,
    )
    pair.start()
    top, bottom = pl.ds(0, SUBLANES), pl.ds(ny - SUBLANES, SUBLANES)
    halos = []
    for i, (src, dst, device) in enumerate(
        [
            (yb, rya, (me_r, col_at(1))),
            (yt, ryb, (me_r, col_at(-1))),
            (xr, rxl, (row_at(1), me_c)),
            (xl, rxr, (row_at(-1), me_c)),
            (xr.at[bottom], rc.at[0], (row_at(1), col_at(1))),
            (xl.at[bottom], rc.at[1], (row_at(-1), col_at(1))),
            (xr.at[top], rc.at[2], (row_at(1), col_at(-1))),
            (xl.at[top], rc.at[3], (row_at(-1), col_at(-1))),
        ]
    ):
        halos.append(
            pltpu.make_async_remote_copy(
                src_ref=src, dst_ref=dst, send_sem=halo_send.at[i], recv_sem=halo_recv.at[i],
                device_id=device, device_id_type=MESH,
            )
        )
        halos[i].start()

    pair.wait_recv()
    both[...] = jnp.maximum(mine[...], theirs[...])

    def tell(d, peer):
        pltpu.make_async_remote_copy(
            src_ref=both, dst_ref=others.at[d - 1], send_sem=peak_send, recv_sem=peak_recv,
            device_id=peer, device_id_type=MESH,
        ).start()

    for_chips(tell)

    up, down = shifts(nx, 1)

    def sweep_tile(at):
        profiles, _ = primitives([u[f, at, :] for f in range(5)])
        for f, difference in enumerate(flux_differences(profiles, up, down, 1)):
            df[f, at, :] = difference

    @pl.loop(0, ny // SUBLANES)
    def _(tile):
        sweep_tile(pl.ds(pl.multiple_of(tile * SUBLANES, SUBLANES), SUBLANES))

    for copy in halos:
        copy.wait_recv()
    for f in range(5):
        u[f, ny : ny + 3, :] = ryb[3 * f : 3 * f + 3, :]
        u[f, ny + 3 : ny + 5, :] = u[f, 3:5, :]
        u[f, ny + 5 : ny + 8, :] = rya[3 * f : 3 * f + 3, :]
    sweep_tile(pl.ds(ny, SUBLANES))

    total = ny + SUBLANES
    lane = lax.broadcasted_iota(jnp.int32, (total, LANES), 1)
    below = lax.broadcasted_iota(jnp.int32, (SUBLANES, LANES), 0) < 4
    far_left = jnp.concatenate([rxl[...], jnp.where(below, rc[2], rc[0])], axis=0)
    far_right = jnp.concatenate([rxr[...], jnp.where(below, rc[3], rc[1])], axis=0)
    seam = []
    for f in range(5):
        begin = u[f, :, 0:LANES]
        end = pltpu.roll(u[f, :, nx - LANES : nx], 64, 1)
        before = pltpu.roll(far_left, 125 - 8 * f, 1)
        after = pltpu.roll(far_right, 64 - 8 * f, 1)
        tile = jnp.where(lane < 32, begin, end)
        tile = jnp.where(lane >= 125, before, tile)
        seam.append(jnp.where((lane >= 64) & (lane < 67), after, tile))
    profiles, _ = primitives(seam)
    up, down = shifts(LANES, 1)
    for f, difference in enumerate(flux_differences(profiles, up, down, 1)):
        df[f, :, 0:LANES] = jnp.where(lane < 3, difference, df[f, :, 0:LANES])
        df[f, :, nx - LANES : nx] = jnp.where(
            lane >= 125, pltpu.roll(difference, 64, 1), df[f, :, nx - LANES : nx]
        )

    pltpu.make_async_copy(others, others, peak_recv).wait()
    peak = jnp.maximum(both[...], jnp.max(others[...], axis=0))
    peak = jnp.max(peak, axis=1, keepdims=True)
    half_step = (0.5 * COURANT) / peak

    up, down = shifts(total, 0)

    @pl.loop(0, nx // LANES)
    def _(chunk):
        at = pl.ds(pl.multiple_of(chunk * LANES, LANES), LANES)
        cells = [u[f, :, at] - half_step * df[f, :, at] for f in range(5)]
        profiles, _ = primitives(cells)
        for f, difference in enumerate(flux_differences(profiles, up, down, 2)):
            result = cells[f] - half_step * difference
            out[f, 0, :, at] = result[0:ny]

    for copy in halos:
        copy.wait_send()
    pair.wait_send()
    pltpu.make_async_copy(others, others, peak_send).wait()


def local(rows, cols, fields):
    ny, nx = fields.shape[2], fields.shape[3]
    vmem = lambda *shape: pltpu.VMEM(shape, jnp.float32)
    dma = pltpu.SemaphoreType.DMA
    return pl.pallas_call(
        functools.partial(kernel, rows, cols),
        out_shape=jax.ShapeDtypeStruct(fields.shape, fields.dtype),
        in_specs=[pl.BlockSpec(memory_space=pltpu.HBM)],
        out_specs=pl.BlockSpec(memory_space=pltpu.VMEM),
        scratch_shapes=[
            vmem(5, ny + SUBLANES, nx),
            vmem(5, ny + SUBLANES, nx),
            vmem(ny, LANES),
            vmem(ny, LANES),
            vmem(16, nx),
            vmem(16, nx),
            vmem(ny, LANES),
            vmem(ny, LANES),
            vmem(16, nx),
            vmem(16, nx),
            vmem(4, SUBLANES, LANES),
            vmem(1, LANES),
            vmem(1, LANES),
            vmem(1, LANES),
            vmem(rows * cols // 2 - 1, 1, LANES),
            dma,
            dma((8,)),
            dma((8,)),
            dma,
            dma,
            dma,
            dma,
        ],
        compiler_params=pltpu.CompilerParams(
            collective_id=0, has_side_effects=True, vmem_limit_bytes=55072 * 1024
        ),
        name="sweeps",
    )(fields)


def solution(mesh):
    spec = P(None, None, "col", "row")
    return jax.shard_map(
        functools.partial(local, mesh.shape["row"], mesh.shape["col"]),
        mesh=mesh,
        in_specs=(spec,),
        out_specs=spec,
        check_vma=False,
    )
```

```python
import functools

import jax
import jax.numpy as jnp
from jax import lax
from jax.experimental import pallas as pl
from jax.experimental.pallas import tpu as pltpu
from jax.sharding import PartitionSpec as P

GAMMA = 1.4
COURANT = 0.3
MESH = pl.DeviceIdType.MESH
LANES = 128
SUBLANES = 8
TINY = 1e-37
UNROLLED = 64


def sound(density, pressure):
    scaled = GAMMA * pressure
    return scaled * lax.rsqrt(jnp.maximum(scaled, TINY)) * lax.rsqrt(density)


def primitives(cells):
    density = cells[0]
    inverse_density = pl.reciprocal(density, approx=True)
    velocity = [cells[k] * inverse_density for k in (1, 2, 3)]
    square = velocity[0] * velocity[0] + velocity[1] * velocity[1] + velocity[2] * velocity[2]
    pressure = (GAMMA - 1.0) * (cells[4] - 0.5 * density * square)
    return [density] + velocity + [pressure]


def limited(first, second):
    return jnp.minimum(jnp.maximum(first, jnp.minimum(second, 0.0)), jnp.maximum(second, 0.0))


def face_values(q, up, down):
    after = up(q)
    jump = after - q
    rise = 0.5 * jump + (1.0 / 12.0) * (down(jump) - up(jump))
    rise = jnp.minimum(jnp.maximum(rise, jnp.minimum(jump, 0.0)), jnp.maximum(jump, 0.0))
    next_fall = jump - rise
    fall, next_rise = down(next_fall), up(rise)
    right = q + limited(rise, fall + fall)
    next_left = after - limited(next_fall, next_rise + next_rise)
    return right, next_left


def flux_differences(profiles, up, down, normal):
    pairs = [face_values(q, up, down) for q in profiles]
    sides = [[pair[side] for pair in pairs] for side in range(2)]
    signal = None
    for density, pressure, speed in [(side[0], side[4], side[normal]) for side in sides]:
        own = jnp.abs(speed) + sound(density, pressure)
        signal = own if signal is None else jnp.maximum(signal, own)
    shifted = [sides[0][normal] + signal, sides[1][normal] - signal]
    mass = [side[0] * speed for side, speed in zip(sides, shifted)]
    fluxes = [mass[0] + mass[1]]
    kinetic = None
    for k in (1, 2, 3):
        left, right = mass[0] * sides[0][k], mass[1] * sides[1][k]
        work = left * sides[0][k] + right * sides[1][k]
        kinetic = work if kinetic is None else kinetic + work
        fluxes.append(left + right)
    fluxes[normal] = fluxes[normal] + (sides[0][4] + sides[1][4])
    energy = 0.5 * kinetic
    for side, speed in zip(sides, shifted):
        energy = energy + side[4] * (speed * (1.0 / (GAMMA - 1.0)) + side[normal])
    fluxes.append(energy)
    return [flux - down(flux) for flux in fluxes]


def shifts(length, axis):
    return (
        lambda a: pltpu.roll(a, length - 1, axis),
        lambda a: pltpu.roll(a, 1, axis),
    )


def kernel(
    rows, cols, x, out, u, df, xr, xl, yt, yb, rxl, rxr, rya, ryb, rc, mine, theirs, both, others,
    in_sem, halo_send, halo_recv, pair_send, pair_recv, peak_send, peak_recv,
):
    ny, nx = x.shape[2], x.shape[3]
    me_r, me_c = lax.axis_index("row"), lax.axis_index("col")

    def row_at(step):
        return lax.rem(me_r + (step % rows), rows)

    def col_at(step):
        return lax.rem(me_c + (step % cols), cols)

    load = pltpu.make_async_copy(x.at[:, 0], u.at[:, pl.ds(0, ny)], in_sem)
    load.start()

    barrier = pltpu.get_barrier_semaphore()
    partner = (me_r, me_c + 1 - 2 * lax.rem(me_c, 2))
    half = cols // 2
    count = rows * half

    def for_chips(act):
        if count <= UNROLLED:
            at_row = [row_at(a) for a in range(rows)]
            at_col = [col_at(2 * b) for b in range(half)]
            for d in range(1, count):
                act(d, (at_row[d // half], at_col[d % half]))
        else:

            @pl.loop(1, count)
            def _(d):
                step = 2 * (d % half)
                act(d, (lax.rem(me_r + d // half, rows), lax.rem(me_c + step, cols)))

    def greet(d, peer):
        pl.semaphore_signal(barrier, inc=1, device_id=peer, device_id_type=MESH)

    near = [(me_r, col_at(b)) for b in (1, -1)]
    near += [(row_at(a), col_at(b)) for a in (1, -1) for b in (1, -1)]
    for peer in near:
        greet(0, peer)
    for_chips(greet)
    load.wait()

    peak = None
    for r in range(0, ny, SUBLANES):
        profiles = primitives([u[f, r : r + SUBLANES, :] for f in range(5)])
        speed = jnp.maximum(jnp.abs(profiles[1]), jnp.abs(profiles[2]))
        speed = speed + sound(profiles[0], profiles[4])
        for c in range(0, nx, LANES):
            part = speed[:, c : c + LANES]
            peak = part if peak is None else jnp.maximum(peak, part)
    mine[...] = jnp.max(peak, axis=0, keepdims=True)

    lane = lax.broadcasted_iota(jnp.int32, (ny, LANES), 1)
    pack_r = pack_l = None
    for f in range(5):
        edge_r = pltpu.roll(u[f, 0:ny, nx - LANES : nx], 8 * f + 3, 1)
        edge_l = u[f, 0:ny, 0:LANES]
        if f:
            edge_l = pltpu.roll(edge_l, 8 * f, 1)
            pack_r = jnp.where(lane < 8 * f, pack_r, edge_r)
            pack_l = jnp.where(lane < 8 * f, pack_l, edge_l)
        else:
            pack_r, pack_l = edge_r, edge_l
    xr[...] = pack_r
    xl[...] = pack_l
    for f in range(5):
        yt[3 * f : 3 * f + 3, :] = u[f, 0:3, :]
        yb[3 * f : 3 * f + 3, :] = u[f, ny - 3 : ny, :]
    yt[15:16, :] = u[0, 0:1, :]
    yb[15:16, :] = u[0, 0:1, :]
    pl.semaphore_wait(barrier, count - 1 + len(near))
    pair = pltpu.make_async_remote_copy(
        src_ref=mine, dst_ref=theirs, send_sem=pair_send, recv_sem=pair_recv,
        device_id=partner, device_id_type=MESH,
    )
    pair.start()
    top, bottom = pl.ds(0, SUBLANES), pl.ds(ny - SUBLANES, SUBLANES)
    halos = []
    for i, (src, dst, device) in enumerate(
        [
            (yb, rya, (me_r, col_at(1))),
            (yt, ryb, (me_r, col_at(-1))),
            (xr, rxl, (row_at(1), me_c)),
            (xl, rxr, (row_at(-1), me_c)),
            (xr.at[bottom], rc.at[0], (row_at(1), col_at(1))),
            (xl.at[bottom], rc.at[1], (row_at(-1), col_at(1))),
            (xr.at[top], rc.at[2], (row_at(1), col_at(-1))),
            (xl.at[top], rc.at[3], (row_at(-1), col_at(-1))),
        ]
    ):
        halos.append(
            pltpu.make_async_remote_copy(
                src_ref=src, dst_ref=dst, send_sem=halo_send.at[i], recv_sem=halo_recv.at[i],
                device_id=device, device_id_type=MESH,
            )
        )
        halos[i].start()

    pair.wait_recv()
    both[...] = jnp.maximum(mine[...], theirs[...])

    def tell(d, peer):
        pltpu.make_async_remote_copy(
            src_ref=both, dst_ref=others.at[d - 1], send_sem=peak_send, recv_sem=peak_recv,
            device_id=peer, device_id_type=MESH,
        ).start()

    for_chips(tell)

    up, down = shifts(nx, 1)

    def sweep_tile(at):
        profiles = primitives([u[f, at, :] for f in range(5)])
        for f, difference in enumerate(flux_differences(profiles, up, down, 1)):
            df[f, at, :] = difference

    @pl.loop(0, ny // SUBLANES)
    def _(tile):
        sweep_tile(pl.ds(pl.multiple_of(tile * SUBLANES, SUBLANES), SUBLANES))

    for copy in halos:
        copy.wait_recv()
    for f in range(5):
        u[f, ny : ny + 3, :] = ryb[3 * f : 3 * f + 3, :]
        u[f, ny + 3 : ny + 5, :] = u[f, 3:5, :]
        u[f, ny + 5 : ny + 8, :] = rya[3 * f : 3 * f + 3, :]
    sweep_tile(pl.ds(ny, SUBLANES))

    total = ny + SUBLANES
    lane = lax.broadcasted_iota(jnp.int32, (total, LANES), 1)
    below = lax.broadcasted_iota(jnp.int32, (SUBLANES, LANES), 0) < 4
    far_left = jnp.concatenate([rxl[...], jnp.where(below, rc[2], rc[0])], axis=0)
    far_right = jnp.concatenate([rxr[...], jnp.where(below, rc[3], rc[1])], axis=0)
    seam = []
    for f in range(5):
        begin = u[f, :, 0:LANES]
        end = pltpu.roll(u[f, :, nx - LANES : nx], 64, 1)
        before = pltpu.roll(far_left, 125 - 8 * f, 1)
        after = pltpu.roll(far_right, 64 - 8 * f, 1)
        tile = jnp.where(lane < 32, begin, end)
        tile = jnp.where(lane >= 125, before, tile)
        seam.append(jnp.where((lane >= 64) & (lane < 67), after, tile))
    profiles = primitives(seam)
    up, down = shifts(LANES, 1)
    for f, difference in enumerate(flux_differences(profiles, up, down, 1)):
        df[f, :, 0:LANES] = jnp.where(lane < 3, difference, df[f, :, 0:LANES])
        df[f, :, nx - LANES : nx] = jnp.where(
            lane >= 125, pltpu.roll(difference, 64, 1), df[f, :, nx - LANES : nx]
        )

    pltpu.make_async_copy(others, others, peak_recv).wait()
    peak = jnp.maximum(both[...], jnp.max(others[...], axis=0))
    peak = jnp.max(peak, axis=1, keepdims=True)
    half_step = (0.5 * COURANT) / peak

    up, down = shifts(total, 0)

    @pl.loop(0, nx // LANES)
    def _(chunk):
        at = pl.ds(pl.multiple_of(chunk * LANES, LANES), LANES)
        cells = [u[f, :, at] - half_step * df[f, :, at] for f in range(5)]
        profiles = primitives(cells)
        for f, difference in enumerate(flux_differences(profiles, up, down, 2)):
            result = cells[f] - half_step * difference
            out[f, 0, :, at] = result[0:ny]

    for copy in halos:
        copy.wait_send()
    pair.wait_send()
    pltpu.make_async_copy(others, others, peak_send).wait()


def local(rows, cols, fields):
    ny, nx = fields.shape[2], fields.shape[3]
    vmem = lambda *shape: pltpu.VMEM(shape, jnp.float32)
    dma = pltpu.SemaphoreType.DMA
    return pl.pallas_call(
        functools.partial(kernel, rows, cols),
        out_shape=jax.ShapeDtypeStruct(fields.shape, fields.dtype),
        in_specs=[pl.BlockSpec(memory_space=pltpu.HBM)],
        out_specs=pl.BlockSpec(memory_space=pltpu.VMEM),
        scratch_shapes=[
            vmem(5, ny + SUBLANES, nx),
            vmem(5, ny + SUBLANES, nx),
            vmem(ny, LANES),
            vmem(ny, LANES),
            vmem(16, nx),
            vmem(16, nx),
            vmem(ny, LANES),
            vmem(ny, LANES),
            vmem(16, nx),
            vmem(16, nx),
            vmem(4, SUBLANES, LANES),
            vmem(1, LANES),
            vmem(1, LANES),
            vmem(1, LANES),
            vmem(rows * cols // 2 - 1, 1, LANES),
            dma,
            dma((8,)),
            dma((8,)),
            dma,
            dma,
            dma,
            dma,
        ],
        compiler_params=pltpu.CompilerParams(
            collective_id=0, has_side_effects=True, vmem_limit_bytes=55072 * 1024
        ),
        name="sweeps",
    )(fields)


def solution(mesh):
    spec = P(None, None, "col", "row")
    return jax.shard_map(
        functools.partial(local, mesh.shape["row"], mesh.shape["col"]),
        mesh=mesh,
        in_specs=(spec,),
        out_specs=spec,
        check_vma=False,
    )
```

```python
import functools

import jax
import jax.numpy as jnp
from jax import lax
from jax.experimental import pallas as pl
from jax.experimental.pallas import tpu as pltpu
from jax.sharding import PartitionSpec as P

GAMMA = 1.4
COURANT = 0.3
MESH = pl.DeviceIdType.MESH
LANES = 128
SUBLANES = 8
TINY = 1e-37
UNROLLED = 64


def sound(density, pressure):
    scaled = GAMMA * pressure
    return scaled * lax.rsqrt(jnp.maximum(scaled, TINY)) * lax.rsqrt(density)


def primitives(cells):
    density = cells[0]
    inverse_density = pl.reciprocal(density, approx=True)
    velocity = [cells[k] * inverse_density for k in (1, 2, 3)]
    square = velocity[0] * velocity[0] + velocity[1] * velocity[1] + velocity[2] * velocity[2]
    pressure = (GAMMA - 1.0) * (cells[4] - 0.5 * density * square)
    return [density] + velocity + [pressure]


def limited(first, second):
    return jnp.minimum(jnp.maximum(first, jnp.minimum(second, 0.0)), jnp.maximum(second, 0.0))


def face_values(q, up, down):
    after = up(q)
    jump = after - q
    rise = 0.5 * jump + (1.0 / 12.0) * (down(jump) - up(jump))
    rise = jnp.minimum(jnp.maximum(rise, jnp.minimum(jump, 0.0)), jnp.maximum(jump, 0.0))
    next_fall = jump - rise
    fall, next_rise = down(next_fall), up(rise)
    right = q + limited(rise, fall + fall)
    next_left = after - limited(next_fall, next_rise + next_rise)
    return right, next_left


def flux_differences(profiles, up, down, normal):
    pairs = [face_values(q, up, down) for q in profiles]
    sides = [[pair[side] for pair in pairs] for side in range(2)]
    signal = None
    for density, pressure, speed in [(side[0], side[4], side[normal]) for side in sides]:
        own = jnp.abs(speed) + sound(density, pressure)
        signal = own if signal is None else jnp.maximum(signal, own)
    shifted = [sides[0][normal] + signal, sides[1][normal] - signal]
    mass = [side[0] * speed for side, speed in zip(sides, shifted)]
    fluxes = [mass[0] + mass[1]]
    kinetic = None
    for k in (1, 2, 3):
        left, right = mass[0] * sides[0][k], mass[1] * sides[1][k]
        work = left * sides[0][k] + right * sides[1][k]
        kinetic = work if kinetic is None else kinetic + work
        fluxes.append(left + right)
    fluxes[normal] = fluxes[normal] + (sides[0][4] + sides[1][4])
    energy = 0.5 * kinetic
    for side, speed in zip(sides, shifted):
        energy = energy + side[4] * (speed * (1.0 / (GAMMA - 1.0)) + side[normal])
    fluxes.append(energy)
    return [flux - down(flux) for flux in fluxes]


def shifts(length, axis):
    return (
        lambda a: pltpu.roll(a, length - 1, axis),
        lambda a: pltpu.roll(a, 1, axis),
    )


def kernel(
    rows, cols, x, out, u, df, xr, xl, yt, yb, rxl, rxr, rya, ryb, rc, mine, theirs, both, others,
    in_sem, halo_send, halo_recv, pair_send, pair_recv, peak_send, peak_recv,
):
    ny, nx = x.shape[2], x.shape[3]
    me_r, me_c = lax.axis_index("row"), lax.axis_index("col")

    def row_at(step):
        return lax.rem(me_r + (step % rows), rows)

    def col_at(step):
        return lax.rem(me_c + (step % cols), cols)

    load = pltpu.make_async_copy(x.at[:, 0], u.at[:, pl.ds(0, ny)], in_sem)
    load.start()

    barrier = pltpu.get_barrier_semaphore()
    partner = (me_r, me_c + 1 - 2 * lax.rem(me_c, 2))
    half = cols // 2
    count = rows * half

    def for_chips(act):
        if count <= UNROLLED:
            at_row = [row_at(a) for a in range(rows)]
            at_col = [col_at(2 * b) for b in range(half)]
            for d in range(1, count):
                act(d, (at_row[d // half], at_col[d % half]))
        else:

            @pl.loop(1, count)
            def _(d):
                step = 2 * (d % half)
                act(d, (lax.rem(me_r + d // half, rows), lax.rem(me_c + step, cols)))

    def greet(d, peer):
        pl.semaphore_signal(barrier, inc=1, device_id=peer, device_id_type=MESH)

    near = [(me_r, col_at(b)) for b in (1, -1)]
    near += [(row_at(a), col_at(b)) for a in (1, -1) for b in (1, -1)]
    for peer in near:
        greet(0, peer)
    for_chips(greet)
    load.wait()

    peak = None
    for r in range(0, ny, SUBLANES):
        profiles = primitives([u[f, r : r + SUBLANES, :] for f in range(5)])
        speed = jnp.maximum(jnp.abs(profiles[1]), jnp.abs(profiles[2]))
        speed = speed + sound(profiles[0], profiles[4])
        for c in range(0, nx, LANES):
            part = speed[:, c : c + LANES]
            peak = part if peak is None else jnp.maximum(peak, part)
    mine[...] = jnp.max(peak, axis=0, keepdims=True)

    lane = lax.broadcasted_iota(jnp.int32, (ny, LANES), 1)
    pack_r = pack_l = None
    for f in range(5):
        edge_r = pltpu.roll(u[f, 0:ny, nx - LANES : nx], 8 * f + 3, 1)
        edge_l = u[f, 0:ny, 0:LANES]
        if f:
            edge_l = pltpu.roll(edge_l, 8 * f, 1)
            pack_r = jnp.where(lane < 8 * f, pack_r, edge_r)
            pack_l = jnp.where(lane < 8 * f, pack_l, edge_l)
        else:
            pack_r, pack_l = edge_r, edge_l
    xr[...] = pack_r
    xl[...] = pack_l
    for f in range(5):
        yt[3 * f : 3 * f + 3, :] = u[f, 0:3, :]
        yb[3 * f : 3 * f + 3, :] = u[f, ny - 3 : ny, :]
    yt[15:16, :] = u[0, 0:1, :]
    yb[15:16, :] = u[0, 0:1, :]
    pl.semaphore_wait(barrier, count - 1 + len(near))
    pair = pltpu.make_async_remote_copy(
        src_ref=mine, dst_ref=theirs, send_sem=pair_send, recv_sem=pair_recv,
        device_id=partner, device_id_type=MESH,
    )
    pair.start()
    top, bottom = pl.ds(0, SUBLANES), pl.ds(ny - SUBLANES, SUBLANES)
    halos = []
    for i, (src, dst, device) in enumerate(
        [
            (yb, rya, (me_r, col_at(1))),
            (yt, ryb, (me_r, col_at(-1))),
            (xr, rxl, (row_at(1), me_c)),
            (xl, rxr, (row_at(-1), me_c)),
            (xr.at[bottom], rc.at[0], (row_at(1), col_at(1))),
            (xl.at[bottom], rc.at[1], (row_at(-1), col_at(1))),
            (xr.at[top], rc.at[2], (row_at(1), col_at(-1))),
            (xl.at[top], rc.at[3], (row_at(-1), col_at(-1))),
        ]
    ):
        halos.append(
            pltpu.make_async_remote_copy(
                src_ref=src, dst_ref=dst, send_sem=halo_send.at[i], recv_sem=halo_recv.at[i],
                device_id=device, device_id_type=MESH,
            )
        )
        halos[i].start()

    pair.wait_recv()
    both[...] = jnp.maximum(mine[...], theirs[...])

    def tell(d, peer):
        pltpu.make_async_remote_copy(
            src_ref=both, dst_ref=others.at[d - 1], send_sem=peak_send, recv_sem=peak_recv,
            device_id=peer, device_id_type=MESH,
        ).start()

    for_chips(tell)

    up, down = shifts(nx, 1)

    def sweep_tile(at):
        profiles = primitives([u[f, at, :] for f in range(5)])
        for f, difference in enumerate(flux_differences(profiles, up, down, 1)):
            df[f, at, :] = difference

    deep = 2 * SUBLANES if ny % (2 * SUBLANES) == 0 else SUBLANES

    @pl.loop(0, ny // deep)
    def _(tile):
        sweep_tile(pl.ds(pl.multiple_of(tile * deep, deep), deep))

    for copy in halos:
        copy.wait_recv()
    for f in range(5):
        u[f, ny : ny + 3, :] = ryb[3 * f : 3 * f + 3, :]
        u[f, ny + 3 : ny + 5, :] = u[f, 3:5, :]
        u[f, ny + 5 : ny + 8, :] = rya[3 * f : 3 * f + 3, :]
    sweep_tile(pl.ds(ny, SUBLANES))

    total = ny + SUBLANES
    lane = lax.broadcasted_iota(jnp.int32, (total, LANES), 1)
    below = lax.broadcasted_iota(jnp.int32, (SUBLANES, LANES), 0) < 4
    far_left = jnp.concatenate([rxl[...], jnp.where(below, rc[2], rc[0])], axis=0)
    far_right = jnp.concatenate([rxr[...], jnp.where(below, rc[3], rc[1])], axis=0)
    seam = []
    for f in range(5):
        begin = u[f, :, 0:LANES]
        end = pltpu.roll(u[f, :, nx - LANES : nx], 64, 1)
        before = pltpu.roll(far_left, 125 - 8 * f, 1)
        after = pltpu.roll(far_right, 64 - 8 * f, 1)
        tile = jnp.where(lane < 32, begin, end)
        tile = jnp.where(lane >= 125, before, tile)
        seam.append(jnp.where((lane >= 64) & (lane < 67), after, tile))
    profiles = primitives(seam)
    up, down = shifts(LANES, 1)
    for f, difference in enumerate(flux_differences(profiles, up, down, 1)):
        df[f, :, 0:LANES] = jnp.where(lane < 3, difference, df[f, :, 0:LANES])
        df[f, :, nx - LANES : nx] = jnp.where(
            lane >= 125, pltpu.roll(difference, 64, 1), df[f, :, nx - LANES : nx]
        )

    pltpu.make_async_copy(others, others, peak_recv).wait()
    peak = jnp.maximum(both[...], jnp.max(others[...], axis=0))
    peak = jnp.max(peak, axis=1, keepdims=True)
    half_step = (0.5 * COURANT) / peak

    up, down = shifts(total, 0)

    wide = 2 * LANES if nx % (2 * LANES) == 0 else LANES

    @pl.loop(0, nx // wide)
    def _(chunk):
        at = pl.ds(pl.multiple_of(chunk * wide, wide), wide)
        cells = [u[f, :, at] - half_step * df[f, :, at] for f in range(5)]
        profiles = primitives(cells)
        for f, difference in enumerate(flux_differences(profiles, up, down, 2)):
            result = cells[f] - half_step * difference
            out[f, 0, :, at] = result[0:ny]

    for copy in halos:
        copy.wait_send()
    pair.wait_send()
    pltpu.make_async_copy(others, others, peak_send).wait()


def local(rows, cols, fields):
    ny, nx = fields.shape[2], fields.shape[3]
    vmem = lambda *shape: pltpu.VMEM(shape, jnp.float32)
    dma = pltpu.SemaphoreType.DMA
    return pl.pallas_call(
        functools.partial(kernel, rows, cols),
        out_shape=jax.ShapeDtypeStruct(fields.shape, fields.dtype),
        in_specs=[pl.BlockSpec(memory_space=pltpu.HBM)],
        out_specs=pl.BlockSpec(memory_space=pltpu.VMEM),
        scratch_shapes=[
            vmem(5, ny + SUBLANES, nx),
            vmem(5, ny + SUBLANES, nx),
            vmem(ny, LANES),
            vmem(ny, LANES),
            vmem(16, nx),
            vmem(16, nx),
            vmem(ny, LANES),
            vmem(ny, LANES),
            vmem(16, nx),
            vmem(16, nx),
            vmem(4, SUBLANES, LANES),
            vmem(1, LANES),
            vmem(1, LANES),
            vmem(1, LANES),
            vmem(rows * cols // 2 - 1, 1, LANES),
            dma,
            dma((8,)),
            dma((8,)),
            dma,
            dma,
            dma,
            dma,
        ],
        compiler_params=pltpu.CompilerParams(
            collective_id=0, has_side_effects=True, vmem_limit_bytes=55072 * 1024
        ),
        name="sweeps",
    )(fields)


def solution(mesh):
    spec = P(None, None, "col", "row")
    return jax.shard_map(
        functools.partial(local, mesh.shape["row"], mesh.shape["col"]),
        mesh=mesh,
        in_specs=(spec,),
        out_specs=spec,
        check_vma=False,
    )
```

```python
import functools

import jax
import jax.numpy as jnp
from jax import lax
from jax.experimental import pallas as pl
from jax.experimental.pallas import tpu as pltpu
from jax.sharding import PartitionSpec as P

GAMMA = 1.4
COURANT = 0.3
MESH = pl.DeviceIdType.MESH
LANES = 128
SUBLANES = 8
TINY = 1e-37
UNROLLED = 64


def sound(density, pressure):
    scaled = GAMMA * pressure
    return scaled * lax.rsqrt(jnp.maximum(scaled, TINY)) * lax.rsqrt(density)


def primitives(cells):
    density = cells[0]
    inverse_density = pl.reciprocal(density, approx=True)
    velocity = [cells[k] * inverse_density for k in (1, 2, 3)]
    square = velocity[0] * velocity[0] + velocity[1] * velocity[1] + velocity[2] * velocity[2]
    pressure = (GAMMA - 1.0) * (cells[4] - 0.5 * density * square)
    return [density] + velocity + [pressure]


def limited(first, second):
    return jnp.minimum(jnp.maximum(first, jnp.minimum(second, 0.0)), jnp.maximum(second, 0.0))


def face_values(q, up, down):
    after = up(q)
    jump = after - q
    rise = 0.5 * jump + (1.0 / 12.0) * (down(jump) - up(jump))
    rise = jnp.minimum(jnp.maximum(rise, jnp.minimum(jump, 0.0)), jnp.maximum(jump, 0.0))
    next_fall = jump - rise
    fall, next_rise = down(next_fall), up(rise)
    right = q + limited(rise, fall + fall)
    next_left = after - limited(next_fall, next_rise + next_rise)
    return right, next_left


def flux_differences(profiles, up, down, normal):
    pairs = [face_values(q, up, down) for q in profiles]
    sides = [[pair[side] for pair in pairs] for side in range(2)]
    signal = None
    for density, pressure, speed in [(side[0], side[4], side[normal]) for side in sides]:
        own = jnp.abs(speed) + sound(density, pressure)
        signal = own if signal is None else jnp.maximum(signal, own)
    shifted = [sides[0][normal] + signal, sides[1][normal] - signal]
    mass = [side[0] * speed for side, speed in zip(sides, shifted)]
    fluxes = [mass[0] + mass[1]]
    kinetic = None
    for k in (1, 2, 3):
        left, right = mass[0] * sides[0][k], mass[1] * sides[1][k]
        work = left * sides[0][k] + right * sides[1][k]
        kinetic = work if kinetic is None else kinetic + work
        fluxes.append(left + right)
    fluxes[normal] = fluxes[normal] + (sides[0][4] + sides[1][4])
    energy = 0.5 * kinetic
    for side, speed in zip(sides, shifted):
        energy = energy + side[4] * (speed * (1.0 / (GAMMA - 1.0)) + side[normal])
    fluxes.append(energy)
    return [flux - down(flux) for flux in fluxes]


def shifts(length, axis):
    return (
        lambda a: pltpu.roll(a, length - 1, axis),
        lambda a: pltpu.roll(a, 1, axis),
    )


def kernel(
    rows, cols, x, out, u, df, xr, xl, yt, yb, rxl, rxr, rya, ryb, rc, mine, theirs, both, others,
    in_sem, halo_send, halo_recv, pair_send, pair_recv, peak_send, peak_recv,
):
    ny, nx = x.shape[2], x.shape[3]
    me_r, me_c = lax.axis_index("row"), lax.axis_index("col")

    def row_at(step):
        return lax.rem(me_r + (step % rows), rows)

    def col_at(step):
        return lax.rem(me_c + (step % cols), cols)

    load = pltpu.make_async_copy(x.at[:, 0], u.at[:, pl.ds(0, ny)], in_sem)
    load.start()

    barrier = pltpu.get_barrier_semaphore()
    partner = (me_r, me_c + 1 - 2 * lax.rem(me_c, 2))
    half = cols // 2
    count = rows * half

    def for_chips(act):
        if count <= UNROLLED:
            at_row = [row_at(a) for a in range(rows)]
            at_col = [col_at(2 * b) for b in range(half)]
            for d in range(1, count):
                act(d, (at_row[d // half], at_col[d % half]))
        else:

            @pl.loop(1, count)
            def _(d):
                step = 2 * (d % half)
                act(d, (lax.rem(me_r + d // half, rows), lax.rem(me_c + step, cols)))

    def greet(d, peer):
        pl.semaphore_signal(barrier, inc=1, device_id=peer, device_id_type=MESH)

    near = [(me_r, col_at(b)) for b in (1, -1)]
    near += [(row_at(a), col_at(b)) for a in (1, -1) for b in (1, -1)]
    for peer in near:
        greet(0, peer)
    for_chips(greet)
    load.wait()

    peak = None
    for r in range(0, ny, SUBLANES):
        profiles = primitives([u[f, r : r + SUBLANES, :] for f in range(5)])
        speed = jnp.maximum(jnp.abs(profiles[1]), jnp.abs(profiles[2]))
        speed = speed + sound(profiles[0], profiles[4])
        for c in range(0, nx, LANES):
            part = speed[:, c : c + LANES]
            peak = part if peak is None else jnp.maximum(peak, part)
    mine[...] = jnp.max(peak, axis=0, keepdims=True)

    pl.semaphore_wait(barrier, count - 1 + len(near))
    pair = pltpu.make_async_remote_copy(
        src_ref=mine, dst_ref=theirs, send_sem=pair_send, recv_sem=pair_recv,
        device_id=partner, device_id_type=MESH,
    )
    pair.start()

    lane = lax.broadcasted_iota(jnp.int32, (ny, LANES), 1)
    pack_r = pack_l = None
    for f in range(5):
        edge_r = pltpu.roll(u[f, 0:ny, nx - LANES : nx], 8 * f + 3, 1)
        edge_l = u[f, 0:ny, 0:LANES]
        if f:
            edge_l = pltpu.roll(edge_l, 8 * f, 1)
            pack_r = jnp.where(lane < 8 * f, pack_r, edge_r)
            pack_l = jnp.where(lane < 8 * f, pack_l, edge_l)
        else:
            pack_r, pack_l = edge_r, edge_l
    xr[...] = pack_r
    xl[...] = pack_l
    for f in range(5):
        yt[3 * f : 3 * f + 3, :] = u[f, 0:3, :]
        yb[3 * f : 3 * f + 3, :] = u[f, ny - 3 : ny, :]
    yt[15:16, :] = u[0, 0:1, :]
    yb[15:16, :] = u[0, 0:1, :]
    top, bottom = pl.ds(0, SUBLANES), pl.ds(ny - SUBLANES, SUBLANES)
    halos = []
    for i, (src, dst, device) in enumerate(
        [
            (yb, rya, (me_r, col_at(1))),
            (yt, ryb, (me_r, col_at(-1))),
            (xr, rxl, (row_at(1), me_c)),
            (xl, rxr, (row_at(-1), me_c)),
            (xr.at[bottom], rc.at[0], (row_at(1), col_at(1))),
            (xl.at[bottom], rc.at[1], (row_at(-1), col_at(1))),
            (xr.at[top], rc.at[2], (row_at(1), col_at(-1))),
            (xl.at[top], rc.at[3], (row_at(-1), col_at(-1))),
        ]
    ):
        halos.append(
            pltpu.make_async_remote_copy(
                src_ref=src, dst_ref=dst, send_sem=halo_send.at[i], recv_sem=halo_recv.at[i],
                device_id=device, device_id_type=MESH,
            )
        )
        halos[i].start()

    pair.wait_recv()
    both[...] = jnp.maximum(mine[...], theirs[...])

    def tell(d, peer):
        pltpu.make_async_remote_copy(
            src_ref=both, dst_ref=others.at[d - 1], send_sem=peak_send, recv_sem=peak_recv,
            device_id=peer, device_id_type=MESH,
        ).start()

    for_chips(tell)

    up, down = shifts(nx, 1)

    def sweep_tile(at):
        profiles = primitives([u[f, at, :] for f in range(5)])
        for f, difference in enumerate(flux_differences(profiles, up, down, 1)):
            df[f, at, :] = difference

    deep = 2 * SUBLANES if ny % (2 * SUBLANES) == 0 else SUBLANES

    @pl.loop(0, ny // deep)
    def _(tile):
        sweep_tile(pl.ds(pl.multiple_of(tile * deep, deep), deep))

    for copy in halos:
        copy.wait_recv()
    for f in range(5):
        u[f, ny : ny + 3, :] = ryb[3 * f : 3 * f + 3, :]
        u[f, ny + 3 : ny + 5, :] = u[f, 3:5, :]
        u[f, ny + 5 : ny + 8, :] = rya[3 * f : 3 * f + 3, :]
    sweep_tile(pl.ds(ny, SUBLANES))

    total = ny + SUBLANES
    lane = lax.broadcasted_iota(jnp.int32, (total, LANES), 1)
    below = lax.broadcasted_iota(jnp.int32, (SUBLANES, LANES), 0) < 4
    far_left = jnp.concatenate([rxl[...], jnp.where(below, rc[2], rc[0])], axis=0)
    far_right = jnp.concatenate([rxr[...], jnp.where(below, rc[3], rc[1])], axis=0)
    seam = []
    for f in range(5):
        begin = u[f, :, 0:LANES]
        end = pltpu.roll(u[f, :, nx - LANES : nx], 64, 1)
        before = pltpu.roll(far_left, 125 - 8 * f, 1)
        after = pltpu.roll(far_right, 64 - 8 * f, 1)
        tile = jnp.where(lane < 32, begin, end)
        tile = jnp.where(lane >= 125, before, tile)
        seam.append(jnp.where((lane >= 64) & (lane < 67), after, tile))
    profiles = primitives(seam)
    up, down = shifts(LANES, 1)
    for f, difference in enumerate(flux_differences(profiles, up, down, 1)):
        df[f, :, 0:LANES] = jnp.where(lane < 3, difference, df[f, :, 0:LANES])
        df[f, :, nx - LANES : nx] = jnp.where(
            lane >= 125, pltpu.roll(difference, 64, 1), df[f, :, nx - LANES : nx]
        )

    pltpu.make_async_copy(others, others, peak_recv).wait()
    peak = jnp.maximum(both[...], jnp.max(others[...], axis=0))
    peak = jnp.max(peak, axis=1, keepdims=True)
    half_step = (0.5 * COURANT) / peak

    up, down = shifts(total, 0)

    wide = 2 * LANES if nx % (2 * LANES) == 0 else LANES

    @pl.loop(0, nx // wide)
    def _(chunk):
        at = pl.ds(pl.multiple_of(chunk * wide, wide), wide)
        cells = [u[f, :, at] - half_step * df[f, :, at] for f in range(5)]
        profiles = primitives(cells)
        for f, difference in enumerate(flux_differences(profiles, up, down, 2)):
            result = cells[f] - half_step * difference
            out[f, 0, :, at] = result[0:ny]

    for copy in halos:
        copy.wait_send()
    pair.wait_send()
    pltpu.make_async_copy(others, others, peak_send).wait()


def local(rows, cols, fields):
    ny, nx = fields.shape[2], fields.shape[3]
    vmem = lambda *shape: pltpu.VMEM(shape, jnp.float32)
    dma = pltpu.SemaphoreType.DMA
    return pl.pallas_call(
        functools.partial(kernel, rows, cols),
        out_shape=jax.ShapeDtypeStruct(fields.shape, fields.dtype),
        in_specs=[pl.BlockSpec(memory_space=pltpu.HBM)],
        out_specs=pl.BlockSpec(memory_space=pltpu.VMEM),
        scratch_shapes=[
            vmem(5, ny + SUBLANES, nx),
            vmem(5, ny + SUBLANES, nx),
            vmem(ny, LANES),
            vmem(ny, LANES),
            vmem(16, nx),
            vmem(16, nx),
            vmem(ny, LANES),
            vmem(ny, LANES),
            vmem(16, nx),
            vmem(16, nx),
            vmem(4, SUBLANES, LANES),
            vmem(1, LANES),
            vmem(1, LANES),
            vmem(1, LANES),
            vmem(rows * cols // 2 - 1, 1, LANES),
            dma,
            dma((8,)),
            dma((8,)),
            dma,
            dma,
            dma,
            dma,
        ],
        compiler_params=pltpu.CompilerParams(
            collective_id=0, has_side_effects=True, vmem_limit_bytes=55072 * 1024
        ),
        name="sweeps",
    )(fields)


def solution(mesh):
    spec = P(None, None, "col", "row")
    return jax.shard_map(
        functools.partial(local, mesh.shape["row"], mesh.shape["col"]),
        mesh=mesh,
        in_specs=(spec,),
        out_specs=spec,
        check_vma=False,
    )
```

```python
import functools

import jax
import jax.numpy as jnp
from jax import lax
from jax.experimental import pallas as pl
from jax.experimental.pallas import tpu as pltpu
from jax.sharding import PartitionSpec as P

GAMMA = 1.4
COURANT = 0.3
MESH = pl.DeviceIdType.MESH
LANES = 128
SUBLANES = 8
TINY = 1e-37
UNROLLED = 64


def sound(density, pressure):
    scaled = GAMMA * pressure
    return scaled * lax.rsqrt(jnp.maximum(scaled, TINY)) * lax.rsqrt(density)


def primitives(cells):
    density = cells[0]
    inverse_density = pl.reciprocal(density, approx=True)
    velocity = [cells[k] * inverse_density for k in (1, 2, 3)]
    square = velocity[0] * velocity[0] + velocity[1] * velocity[1] + velocity[2] * velocity[2]
    pressure = (GAMMA - 1.0) * (cells[4] - 0.5 * density * square)
    return [density] + velocity + [pressure]


def limited(first, second):
    return jnp.minimum(jnp.maximum(first, jnp.minimum(second, 0.0)), jnp.maximum(second, 0.0))


def face_values(q, up, down):
    after = up(q)
    jump = after - q
    rise = 0.5 * jump + (1.0 / 12.0) * (down(jump) - up(jump))
    rise = jnp.minimum(jnp.maximum(rise, jnp.minimum(jump, 0.0)), jnp.maximum(jump, 0.0))
    next_fall = jump - rise
    fall, next_rise = down(next_fall), up(rise)
    right = q + limited(rise, fall + fall)
    next_left = after - limited(next_fall, next_rise + next_rise)
    return right, next_left


def flux_differences(profiles, up, down, normal):
    pairs = [face_values(q, up, down) for q in profiles]
    sides = [[pair[side] for pair in pairs] for side in range(2)]
    signal = None
    for density, pressure, speed in [(side[0], side[4], side[normal]) for side in sides]:
        own = jnp.abs(speed) + sound(density, pressure)
        signal = own if signal is None else jnp.maximum(signal, own)
    shifted = [sides[0][normal] + signal, sides[1][normal] - signal]
    mass = [side[0] * speed for side, speed in zip(sides, shifted)]
    fluxes = [mass[0] + mass[1]]
    kinetic = None
    for k in (1, 2, 3):
        left, right = mass[0] * sides[0][k], mass[1] * sides[1][k]
        work = left * sides[0][k] + right * sides[1][k]
        kinetic = work if kinetic is None else kinetic + work
        fluxes.append(left + right)
    fluxes[normal] = fluxes[normal] + (sides[0][4] + sides[1][4])
    energy = 0.5 * kinetic
    for side, speed in zip(sides, shifted):
        energy = energy + side[4] * (speed * (1.0 / (GAMMA - 1.0)) + side[normal])
    fluxes.append(energy)
    return [flux - down(flux) for flux in fluxes]


def shifts(length, axis):
    return (
        lambda a: pltpu.roll(a, length - 1, axis),
        lambda a: pltpu.roll(a, 1, axis),
    )


def kernel(
    rows, cols, x, out, u, df, xr, xl, yt, yb, rxl, rxr, rya, ryb, rc, mine, theirs, both, others,
    in_sem, halo_send, halo_recv, pair_send, pair_recv, peak_send, peak_recv,
):
    ny, nx = x.shape[2], x.shape[3]
    me_r, me_c = lax.axis_index("row"), lax.axis_index("col")

    def row_at(step):
        return lax.rem(me_r + (step % rows), rows)

    def col_at(step):
        return lax.rem(me_c + (step % cols), cols)

    load = pltpu.make_async_copy(x.at[:, 0], u.at[:, pl.ds(0, ny)], in_sem)
    load.start()

    barrier = pltpu.get_barrier_semaphore()
    partner = (me_r, me_c + 1 - 2 * lax.rem(me_c, 2))
    half = cols // 2
    count = rows * half

    def for_chips(act):
        if count <= UNROLLED:
            at_row = [row_at(a) for a in range(rows)]
            at_col = [col_at(2 * b) for b in range(half)]
            for d in range(1, count):
                act(d, (at_row[d // half], at_col[d % half]))
        else:

            @pl.loop(1, count)
            def _(d):
                step = 2 * (d % half)
                act(d, (lax.rem(me_r + d // half, rows), lax.rem(me_c + step, cols)))

    def greet(d, peer):
        pl.semaphore_signal(barrier, inc=1, device_id=peer, device_id_type=MESH)

    near = [(me_r, col_at(b)) for b in (1, -1)]
    near += [(row_at(a), col_at(b)) for a in (1, -1) for b in (1, -1)]
    for peer in near:
        greet(0, peer)
    for_chips(greet)
    load.wait()

    peak = None
    for r in range(0, ny, SUBLANES):
        profiles = primitives([u[f, r : r + SUBLANES, :] for f in range(5)])
        speed = jnp.maximum(jnp.abs(profiles[1]), jnp.abs(profiles[2]))
        speed = speed + sound(profiles[0], profiles[4])
        for c in range(0, nx, LANES):
            part = speed[:, c : c + LANES]
            peak = part if peak is None else jnp.maximum(peak, part)
    mine[...] = jnp.max(peak, axis=0, keepdims=True)

    lane = lax.broadcasted_iota(jnp.int32, (ny, LANES), 1)
    pack_r = pack_l = None
    for f in range(5):
        edge_r = pltpu.roll(u[f, 0:ny, nx - LANES : nx], 8 * f + 3, 1)
        edge_l = u[f, 0:ny, 0:LANES]
        if f:
            edge_l = pltpu.roll(edge_l, 8 * f, 1)
            pack_r = jnp.where(lane < 8 * f, pack_r, edge_r)
            pack_l = jnp.where(lane < 8 * f, pack_l, edge_l)
        else:
            pack_r, pack_l = edge_r, edge_l
    xr[...] = pack_r
    xl[...] = pack_l
    for f in range(5):
        yt[3 * f : 3 * f + 3, :] = u[f, 0:3, :]
        yb[3 * f : 3 * f + 3, :] = u[f, ny - 3 : ny, :]
    yt[15:16, :] = u[0, 0:1, :]
    yb[15:16, :] = u[0, 0:1, :]
    up, down = shifts(nx, 1)

    def sweep_tile(at):
        profiles = primitives([u[f, at, :] for f in range(5)])
        for f, difference in enumerate(flux_differences(profiles, up, down, 1)):
            df[f, at, :] = difference

    deep = 2 * SUBLANES if ny % (2 * SUBLANES) == 0 else SUBLANES

    @pl.loop(0, ny // deep)
    def _(tile):
        sweep_tile(pl.ds(pl.multiple_of(tile * deep, deep), deep))

    pl.semaphore_wait(barrier, count - 1 + len(near))
    pair = pltpu.make_async_remote_copy(
        src_ref=mine, dst_ref=theirs, send_sem=pair_send, recv_sem=pair_recv,
        device_id=partner, device_id_type=MESH,
    )
    pair.start()
    top, bottom = pl.ds(0, SUBLANES), pl.ds(ny - SUBLANES, SUBLANES)
    halos = []
    for i, (src, dst, device) in enumerate(
        [
            (yb, rya, (me_r, col_at(1))),
            (yt, ryb, (me_r, col_at(-1))),
            (xr, rxl, (row_at(1), me_c)),
            (xl, rxr, (row_at(-1), me_c)),
            (xr.at[bottom], rc.at[0], (row_at(1), col_at(1))),
            (xl.at[bottom], rc.at[1], (row_at(-1), col_at(1))),
            (xr.at[top], rc.at[2], (row_at(1), col_at(-1))),
            (xl.at[top], rc.at[3], (row_at(-1), col_at(-1))),
        ]
    ):
        halos.append(
            pltpu.make_async_remote_copy(
                src_ref=src, dst_ref=dst, send_sem=halo_send.at[i], recv_sem=halo_recv.at[i],
                device_id=device, device_id_type=MESH,
            )
        )
        halos[i].start()

    pair.wait_recv()
    both[...] = jnp.maximum(mine[...], theirs[...])

    def tell(d, peer):
        pltpu.make_async_remote_copy(
            src_ref=both, dst_ref=others.at[d - 1], send_sem=peak_send, recv_sem=peak_recv,
            device_id=peer, device_id_type=MESH,
        ).start()

    for_chips(tell)

    for copy in halos:
        copy.wait_recv()
    for f in range(5):
        u[f, ny : ny + 3, :] = ryb[3 * f : 3 * f + 3, :]
        u[f, ny + 3 : ny + 5, :] = u[f, 3:5, :]
        u[f, ny + 5 : ny + 8, :] = rya[3 * f : 3 * f + 3, :]
    sweep_tile(pl.ds(ny, SUBLANES))

    total = ny + SUBLANES
    lane = lax.broadcasted_iota(jnp.int32, (total, LANES), 1)
    below = lax.broadcasted_iota(jnp.int32, (SUBLANES, LANES), 0) < 4
    far_left = jnp.concatenate([rxl[...], jnp.where(below, rc[2], rc[0])], axis=0)
    far_right = jnp.concatenate([rxr[...], jnp.where(below, rc[3], rc[1])], axis=0)
    seam = []
    for f in range(5):
        begin = u[f, :, 0:LANES]
        end = pltpu.roll(u[f, :, nx - LANES : nx], 64, 1)
        before = pltpu.roll(far_left, 125 - 8 * f, 1)
        after = pltpu.roll(far_right, 64 - 8 * f, 1)
        tile = jnp.where(lane < 32, begin, end)
        tile = jnp.where(lane >= 125, before, tile)
        seam.append(jnp.where((lane >= 64) & (lane < 67), after, tile))
    profiles = primitives(seam)
    up, down = shifts(LANES, 1)
    for f, difference in enumerate(flux_differences(profiles, up, down, 1)):
        df[f, :, 0:LANES] = jnp.where(lane < 3, difference, df[f, :, 0:LANES])
        df[f, :, nx - LANES : nx] = jnp.where(
            lane >= 125, pltpu.roll(difference, 64, 1), df[f, :, nx - LANES : nx]
        )

    pltpu.make_async_copy(others, others, peak_recv).wait()
    peak = jnp.maximum(both[...], jnp.max(others[...], axis=0))
    peak = jnp.max(peak, axis=1, keepdims=True)
    half_step = (0.5 * COURANT) / peak

    up, down = shifts(total, 0)

    wide = 2 * LANES if nx % (2 * LANES) == 0 else LANES

    @pl.loop(0, nx // wide)
    def _(chunk):
        at = pl.ds(pl.multiple_of(chunk * wide, wide), wide)
        cells = [u[f, :, at] - half_step * df[f, :, at] for f in range(5)]
        profiles = primitives(cells)
        for f, difference in enumerate(flux_differences(profiles, up, down, 2)):
            result = cells[f] - half_step * difference
            out[f, 0, :, at] = result[0:ny]

    for copy in halos:
        copy.wait_send()
    pair.wait_send()
    pltpu.make_async_copy(others, others, peak_send).wait()


def local(rows, cols, fields):
    ny, nx = fields.shape[2], fields.shape[3]
    vmem = lambda *shape: pltpu.VMEM(shape, jnp.float32)
    dma = pltpu.SemaphoreType.DMA
    return pl.pallas_call(
        functools.partial(kernel, rows, cols),
        out_shape=jax.ShapeDtypeStruct(fields.shape, fields.dtype),
        in_specs=[pl.BlockSpec(memory_space=pltpu.HBM)],
        out_specs=pl.BlockSpec(memory_space=pltpu.VMEM),
        scratch_shapes=[
            vmem(5, ny + SUBLANES, nx),
            vmem(5, ny + SUBLANES, nx),
            vmem(ny, LANES),
            vmem(ny, LANES),
            vmem(16, nx),
            vmem(16, nx),
            vmem(ny, LANES),
            vmem(ny, LANES),
            vmem(16, nx),
            vmem(16, nx),
            vmem(4, SUBLANES, LANES),
            vmem(1, LANES),
            vmem(1, LANES),
            vmem(1, LANES),
            vmem(rows * cols // 2 - 1, 1, LANES),
            dma,
            dma((8,)),
            dma((8,)),
            dma,
            dma,
            dma,
            dma,
        ],
        compiler_params=pltpu.CompilerParams(
            collective_id=0, has_side_effects=True, vmem_limit_bytes=55072 * 1024
        ),
        name="sweeps",
    )(fields)


def solution(mesh):
    spec = P(None, None, "col", "row")
    return jax.shard_map(
        functools.partial(local, mesh.shape["row"], mesh.shape["col"]),
        mesh=mesh,
        in_specs=(spec,),
        out_specs=spec,
        check_vma=False,
    )
```

```python
import functools

import jax
import jax.numpy as jnp
from jax import lax
from jax.experimental import pallas as pl
from jax.experimental.pallas import tpu as pltpu
from jax.sharding import PartitionSpec as P

GAMMA = 1.4
COURANT = 0.3
MESH = pl.DeviceIdType.MESH
LANES = 128
SUBLANES = 8
TINY = 1e-37
UNROLLED = 64


def sound(density, pressure):
    scaled = GAMMA * pressure
    return scaled * lax.rsqrt(jnp.maximum(scaled, TINY)) * lax.rsqrt(density)


def primitives(cells):
    density = cells[0]
    inverse_density = pl.reciprocal(density, approx=True)
    velocity = [cells[k] * inverse_density for k in (1, 2, 3)]
    square = velocity[0] * velocity[0] + velocity[1] * velocity[1] + velocity[2] * velocity[2]
    pressure = (GAMMA - 1.0) * (cells[4] - 0.5 * density * square)
    return [density] + velocity + [pressure]


def limited(first, second):
    return jnp.minimum(jnp.maximum(first, jnp.minimum(second, 0.0)), jnp.maximum(second, 0.0))


def face_values(q, up, down):
    after = up(q)
    jump = after - q
    rise = 0.5 * jump + (1.0 / 12.0) * (down(jump) - up(jump))
    rise = jnp.minimum(jnp.maximum(rise, jnp.minimum(jump, 0.0)), jnp.maximum(jump, 0.0))
    next_fall = jump - rise
    fall, next_rise = down(next_fall), up(rise)
    right = q + limited(rise, fall + fall)
    next_left = after - limited(next_fall, next_rise + next_rise)
    return right, next_left


def flux_differences(profiles, up, down, normal):
    pairs = [face_values(q, up, down) for q in profiles]
    sides = [[pair[side] for pair in pairs] for side in range(2)]
    signal = None
    for density, pressure, speed in [(side[0], side[4], side[normal]) for side in sides]:
        own = jnp.abs(speed) + sound(density, pressure)
        signal = own if signal is None else jnp.maximum(signal, own)
    shifted = [sides[0][normal] + signal, sides[1][normal] - signal]
    mass = [side[0] * speed for side, speed in zip(sides, shifted)]
    fluxes = [mass[0] + mass[1]]
    kinetic = None
    for k in (1, 2, 3):
        left, right = mass[0] * sides[0][k], mass[1] * sides[1][k]
        work = left * sides[0][k] + right * sides[1][k]
        kinetic = work if kinetic is None else kinetic + work
        fluxes.append(left + right)
    fluxes[normal] = fluxes[normal] + (sides[0][4] + sides[1][4])
    energy = 0.5 * kinetic
    for side, speed in zip(sides, shifted):
        energy = energy + side[4] * (speed * (1.0 / (GAMMA - 1.0)) + side[normal])
    fluxes.append(energy)
    return [flux - down(flux) for flux in fluxes]


def shifts(length, axis):
    return (
        lambda a: pltpu.roll(a, length - 1, axis),
        lambda a: pltpu.roll(a, 1, axis),
    )


def kernel(
    rows, cols, x, out, u, df, xr, xl, yt, yb, rxl, rxr, rya, ryb, rc, mine, others,
    in_sem, halo_send, halo_recv, peak_send, peak_recv,
):
    ny, nx = x.shape[2], x.shape[3]
    me_r, me_c = lax.axis_index("row"), lax.axis_index("col")

    def row_at(step):
        return lax.rem(me_r + (step % rows), rows)

    def col_at(step):
        return lax.rem(me_c + (step % cols), cols)

    load = pltpu.make_async_copy(x.at[:, 0], u.at[:, pl.ds(0, ny)], in_sem)
    load.start()

    barrier = pltpu.get_barrier_semaphore()
    count = rows * cols

    def for_peers(act):
        if count <= UNROLLED:
            at_row = [row_at(a) for a in range(rows)]
            at_col = [col_at(b) for b in range(cols)]
            for d in range(1, count):
                act(d, (at_row[d // cols], at_col[d % cols]))
        else:

            @pl.loop(1, count)
            def _(d):
                act(d, (lax.rem(me_r + d // cols, rows), lax.rem(me_c + d % cols, cols)))

    def greet(d, peer):
        pl.semaphore_signal(barrier, inc=1, device_id=peer, device_id_type=MESH)

    for_peers(greet)
    load.wait()

    peak = None
    for r in range(0, ny, SUBLANES):
        profiles = primitives([u[f, r : r + SUBLANES, :] for f in range(5)])
        speed = jnp.maximum(jnp.abs(profiles[1]), jnp.abs(profiles[2]))
        speed = speed + sound(profiles[0], profiles[4])
        for c in range(0, nx, LANES):
            part = speed[:, c : c + LANES]
            peak = part if peak is None else jnp.maximum(peak, part)
    peak = jnp.max(jnp.max(peak, axis=0, keepdims=True), axis=1, keepdims=True)
    mine[...] = jnp.broadcast_to(peak, mine.shape)

    lane = lax.broadcasted_iota(jnp.int32, (ny, LANES), 1)
    pack_r = pack_l = None
    for f in range(5):
        edge_r = pltpu.roll(u[f, 0:ny, nx - LANES : nx], 8 * f + 3, 1)
        edge_l = u[f, 0:ny, 0:LANES]
        if f:
            edge_l = pltpu.roll(edge_l, 8 * f, 1)
            pack_r = jnp.where(lane < 8 * f, pack_r, edge_r)
            pack_l = jnp.where(lane < 8 * f, pack_l, edge_l)
        else:
            pack_r, pack_l = edge_r, edge_l
    xr[...] = pack_r
    xl[...] = pack_l
    for f in range(5):
        yt[3 * f : 3 * f + 3, :] = u[f, 0:3, :]
        yb[3 * f : 3 * f + 3, :] = u[f, ny - 3 : ny, :]
    yt[15:16, :] = u[0, 0:1, :]
    yb[15:16, :] = u[0, 0:1, :]
    pl.semaphore_wait(barrier, count - 1)

    def tell(d, peer):
        pltpu.make_async_remote_copy(
            src_ref=mine, dst_ref=others.at[d - 1], send_sem=peak_send, recv_sem=peak_recv,
            device_id=peer, device_id_type=MESH,
        ).start()

    for_peers(tell)
    top, bottom = pl.ds(0, SUBLANES), pl.ds(ny - SUBLANES, SUBLANES)
    halos = []
    for i, (src, dst, device) in enumerate(
        [
            (yb, rya, (me_r, col_at(1))),
            (yt, ryb, (me_r, col_at(-1))),
            (xr, rxl, (row_at(1), me_c)),
            (xl, rxr, (row_at(-1), me_c)),
            (xr.at[bottom], rc.at[0], (row_at(1), col_at(1))),
            (xl.at[bottom], rc.at[1], (row_at(-1), col_at(1))),
            (xr.at[top], rc.at[2], (row_at(1), col_at(-1))),
            (xl.at[top], rc.at[3], (row_at(-1), col_at(-1))),
        ]
    ):
        halos.append(
            pltpu.make_async_remote_copy(
                src_ref=src, dst_ref=dst, send_sem=halo_send.at[i], recv_sem=halo_recv.at[i],
                device_id=device, device_id_type=MESH,
            )
        )
        halos[i].start()

    up, down = shifts(nx, 1)

    def sweep_tile(at):
        profiles = primitives([u[f, at, :] for f in range(5)])
        for f, difference in enumerate(flux_differences(profiles, up, down, 1)):
            df[f, at, :] = difference

    deep = 2 * SUBLANES if ny % (2 * SUBLANES) == 0 else SUBLANES

    @pl.loop(0, ny // deep)
    def _(tile):
        sweep_tile(pl.ds(pl.multiple_of(tile * deep, deep), deep))

    for copy in halos:
        copy.wait_recv()
    for f in range(5):
        u[f, ny : ny + 3, :] = ryb[3 * f : 3 * f + 3, :]
        u[f, ny + 3 : ny + 5, :] = u[f, 3:5, :]
        u[f, ny + 5 : ny + 8, :] = rya[3 * f : 3 * f + 3, :]
    sweep_tile(pl.ds(ny, SUBLANES))

    total = ny + SUBLANES
    lane = lax.broadcasted_iota(jnp.int32, (total, LANES), 1)
    below = lax.broadcasted_iota(jnp.int32, (SUBLANES, LANES), 0) < 4
    far_left = jnp.concatenate([rxl[...], jnp.where(below, rc[2], rc[0])], axis=0)
    far_right = jnp.concatenate([rxr[...], jnp.where(below, rc[3], rc[1])], axis=0)
    seam = []
    for f in range(5):
        begin = u[f, :, 0:LANES]
        end = pltpu.roll(u[f, :, nx - LANES : nx], 64, 1)
        before = pltpu.roll(far_left, 125 - 8 * f, 1)
        after = pltpu.roll(far_right, 64 - 8 * f, 1)
        tile = jnp.where(lane < 32, begin, end)
        tile = jnp.where(lane >= 125, before, tile)
        seam.append(jnp.where((lane >= 64) & (lane < 67), after, tile))
    profiles = primitives(seam)
    up, down = shifts(LANES, 1)
    for f, difference in enumerate(flux_differences(profiles, up, down, 1)):
        df[f, :, 0:LANES] = jnp.where(lane < 3, difference, df[f, :, 0:LANES])
        df[f, :, nx - LANES : nx] = jnp.where(
            lane >= 125, pltpu.roll(difference, 64, 1), df[f, :, nx - LANES : nx]
        )

    pltpu.make_async_copy(others, others, peak_recv).wait()
    peak = jnp.maximum(mine[...], jnp.max(others[...], axis=0))
    half_step = (0.5 * COURANT) / peak

    up, down = shifts(total, 0)

    wide = 2 * LANES if nx % (2 * LANES) == 0 else LANES
    half_step = jnp.concatenate([half_step] * (wide // LANES), axis=1)

    @pl.loop(0, nx // wide)
    def _(chunk):
        at = pl.ds(pl.multiple_of(chunk * wide, wide), wide)
        cells = [u[f, :, at] - half_step * df[f, :, at] for f in range(5)]
        profiles = primitives(cells)
        for f, difference in enumerate(flux_differences(profiles, up, down, 2)):
            result = cells[f] - half_step * difference
            out[f, 0, :, at] = result[0:ny]

    for copy in halos:
        copy.wait_send()
    pltpu.make_async_copy(others, others, peak_send).wait()


def local(rows, cols, fields):
    ny, nx = fields.shape[2], fields.shape[3]
    vmem = lambda *shape: pltpu.VMEM(shape, jnp.float32)
    dma = pltpu.SemaphoreType.DMA
    return pl.pallas_call(
        functools.partial(kernel, rows, cols),
        out_shape=jax.ShapeDtypeStruct(fields.shape, fields.dtype),
        in_specs=[pl.BlockSpec(memory_space=pltpu.HBM)],
        out_specs=pl.BlockSpec(memory_space=pltpu.VMEM),
        scratch_shapes=[
            vmem(5, ny + SUBLANES, nx),
            vmem(5, ny + SUBLANES, nx),
            vmem(ny, LANES),
            vmem(ny, LANES),
            vmem(16, nx),
            vmem(16, nx),
            vmem(ny, LANES),
            vmem(ny, LANES),
            vmem(16, nx),
            vmem(16, nx),
            vmem(4, SUBLANES, LANES),
            vmem(1, LANES),
            vmem(rows * cols - 1, 1, LANES),
            dma,
            dma((8,)),
            dma((8,)),
            dma,
            dma,
        ],
        compiler_params=pltpu.CompilerParams(
            collective_id=0, has_side_effects=True, vmem_limit_bytes=55072 * 1024
        ),
        name="sweeps",
    )(fields)


def solution(mesh):
    spec = P(None, None, "col", "row")
    return jax.shard_map(
        functools.partial(local, mesh.shape["row"], mesh.shape["col"]),
        mesh=mesh,
        in_specs=(spec,),
        out_specs=spec,
        check_vma=False,
    )
```

```python
import functools

import jax
import jax.numpy as jnp
from jax import lax
from jax.experimental import pallas as pl
from jax.experimental.pallas import tpu as pltpu
from jax.sharding import PartitionSpec as P

GAMMA = 1.4
COURANT = 0.3
MESH = pl.DeviceIdType.MESH
LANES = 128
SUBLANES = 8
TINY = 1e-37
UNROLLED = 64


def sound(density, pressure):
    scaled = GAMMA * pressure
    return scaled * lax.rsqrt(jnp.maximum(scaled, TINY)) * lax.rsqrt(density)


def primitives(cells):
    density = cells[0]
    inverse_density = pl.reciprocal(density, approx=True)
    velocity = [cells[k] * inverse_density for k in (1, 2, 3)]
    square = velocity[0] * velocity[0] + velocity[1] * velocity[1] + velocity[2] * velocity[2]
    pressure = (GAMMA - 1.0) * (cells[4] - 0.5 * density * square)
    return [density] + velocity + [pressure]


def limited(first, second):
    return jnp.minimum(jnp.maximum(first, jnp.minimum(second, 0.0)), jnp.maximum(second, 0.0))


def face_values(q, up, down):
    after = up(q)
    jump = after - q
    rise = 0.5 * jump + (1.0 / 12.0) * (down(jump) - up(jump))
    rise = jnp.minimum(jnp.maximum(rise, jnp.minimum(jump, 0.0)), jnp.maximum(jump, 0.0))
    next_fall = jump - rise
    fall, next_rise = down(next_fall), up(rise)
    right = q + limited(rise, fall + fall)
    next_left = after - limited(next_fall, next_rise + next_rise)
    return right, next_left


def flux_differences(profiles, up, down, normal):
    pairs = [face_values(q, up, down) for q in profiles]
    sides = [[pair[side] for pair in pairs] for side in range(2)]
    signal = None
    for density, pressure, speed in [(side[0], side[4], side[normal]) for side in sides]:
        own = jnp.abs(speed) + sound(density, pressure)
        signal = own if signal is None else jnp.maximum(signal, own)
    shifted = [sides[0][normal] + signal, sides[1][normal] - signal]
    mass = [side[0] * speed for side, speed in zip(sides, shifted)]
    fluxes = [mass[0] + mass[1]]
    kinetic = None
    for k in (1, 2, 3):
        left, right = mass[0] * sides[0][k], mass[1] * sides[1][k]
        work = left * sides[0][k] + right * sides[1][k]
        kinetic = work if kinetic is None else kinetic + work
        fluxes.append(left + right)
    fluxes[normal] = fluxes[normal] + (sides[0][4] + sides[1][4])
    energy = 0.5 * kinetic
    for side, speed in zip(sides, shifted):
        energy = energy + side[4] * (speed * (1.0 / (GAMMA - 1.0)) + side[normal])
    fluxes.append(energy)
    return [flux - down(flux) for flux in fluxes]


def shifts(length, axis):
    return (
        lambda a: pltpu.roll(a, length - 1, axis),
        lambda a: pltpu.roll(a, 1, axis),
    )


def kernel(
    rows, cols, x, out, u, df, xr, xl, yt, yb, rxl, rxr, rya, ryb, rc, mine, others,
    in_sem, halo_send, halo_recv, peak_send, peak_recv,
):
    ny, nx = x.shape[2], x.shape[3]
    me_r, me_c = lax.axis_index("row"), lax.axis_index("col")

    def row_at(step):
        return lax.rem(me_r + (step % rows), rows)

    def col_at(step):
        return lax.rem(me_c + (step % cols), cols)

    load = pltpu.make_async_copy(x.at[:, 0], u.at[:, pl.ds(0, ny)], in_sem)
    load.start()

    barrier = pltpu.get_barrier_semaphore()
    count = rows * cols

    def for_peers(act):
        if count <= UNROLLED:
            at_row = [row_at(a) for a in range(rows)]
            at_col = [col_at(b) for b in range(cols)]
            for d in range(1, count):
                act(d, (at_row[d // cols], at_col[d % cols]))
        else:

            @pl.loop(1, count)
            def _(d):
                act(d, (lax.rem(me_r + d // cols, rows), lax.rem(me_c + d % cols, cols)))

    def greet(d, peer):
        pl.semaphore_signal(barrier, inc=1, device_id=peer, device_id_type=MESH)

    for_peers(greet)
    load.wait()

    peak = None
    for r in range(0, ny, SUBLANES):
        profiles = primitives([u[f, r : r + SUBLANES, :] for f in range(5)])
        speed = jnp.maximum(jnp.abs(profiles[1]), jnp.abs(profiles[2]))
        speed = speed + sound(profiles[0], profiles[4])
        for c in range(0, nx, LANES):
            part = speed[:, c : c + LANES]
            peak = part if peak is None else jnp.maximum(peak, part)
    peak = jnp.max(jnp.max(peak, axis=0, keepdims=True), axis=1, keepdims=True)
    mine[...] = jnp.broadcast_to(peak, mine.shape)

    lane = lax.broadcasted_iota(jnp.int32, (ny, LANES), 1)
    pack_r = pack_l = None
    for f in range(5):
        edge_r = pltpu.roll(u[f, 0:ny, nx - LANES : nx], 8 * f + 3, 1)
        edge_l = u[f, 0:ny, 0:LANES]
        if f:
            edge_l = pltpu.roll(edge_l, 8 * f, 1)
            pack_r = jnp.where(lane < 8 * f, pack_r, edge_r)
            pack_l = jnp.where(lane < 8 * f, pack_l, edge_l)
        else:
            pack_r, pack_l = edge_r, edge_l
    xr[...] = pack_r
    xl[...] = pack_l
    for f in range(5):
        yt[3 * f : 3 * f + 3, :] = u[f, 0:3, :]
        yb[3 * f : 3 * f + 3, :] = u[f, ny - 3 : ny, :]
    yt[15:16, :] = u[0, 0:1, :]
    yb[15:16, :] = u[0, 0:1, :]
    pl.semaphore_wait(barrier, count - 1)

    def tell(d, peer):
        pltpu.make_async_remote_copy(
            src_ref=mine, dst_ref=others.at[d - 1], send_sem=peak_send, recv_sem=peak_recv,
            device_id=peer, device_id_type=MESH,
        ).start()

    top, bottom = pl.ds(0, SUBLANES), pl.ds(ny - SUBLANES, SUBLANES)
    halos = []
    for i, (src, dst, device) in enumerate(
        [
            (yb, rya, (me_r, col_at(1))),
            (yt, ryb, (me_r, col_at(-1))),
            (xr, rxl, (row_at(1), me_c)),
            (xl, rxr, (row_at(-1), me_c)),
            (xr.at[bottom], rc.at[0], (row_at(1), col_at(1))),
            (xl.at[bottom], rc.at[1], (row_at(-1), col_at(1))),
            (xr.at[top], rc.at[2], (row_at(1), col_at(-1))),
            (xl.at[top], rc.at[3], (row_at(-1), col_at(-1))),
        ]
    ):
        halos.append(
            pltpu.make_async_remote_copy(
                src_ref=src, dst_ref=dst, send_sem=halo_send.at[i], recv_sem=halo_recv.at[i],
                device_id=device, device_id_type=MESH,
            )
        )
        halos[i].start()
        if i == 1:
            for_peers(tell)

    up, down = shifts(nx, 1)

    def sweep_tile(at):
        profiles = primitives([u[f, at, :] for f in range(5)])
        for f, difference in enumerate(flux_differences(profiles, up, down, 1)):
            df[f, at, :] = difference

    deep = 2 * SUBLANES if ny % (2 * SUBLANES) == 0 else SUBLANES

    @pl.loop(0, ny // deep)
    def _(tile):
        sweep_tile(pl.ds(pl.multiple_of(tile * deep, deep), deep))

    for copy in halos:
        copy.wait_recv()
    for f in range(5):
        u[f, ny : ny + 3, :] = ryb[3 * f : 3 * f + 3, :]
        u[f, ny + 3 : ny + 5, :] = u[f, 3:5, :]
        u[f, ny + 5 : ny + 8, :] = rya[3 * f : 3 * f + 3, :]
    sweep_tile(pl.ds(ny, SUBLANES))

    total = ny + SUBLANES
    lane = lax.broadcasted_iota(jnp.int32, (total, LANES), 1)
    below = lax.broadcasted_iota(jnp.int32, (SUBLANES, LANES), 0) < 4
    far_left = jnp.concatenate([rxl[...], jnp.where(below, rc[2], rc[0])], axis=0)
    far_right = jnp.concatenate([rxr[...], jnp.where(below, rc[3], rc[1])], axis=0)
    seam = []
    for f in range(5):
        begin = u[f, :, 0:LANES]
        end = pltpu.roll(u[f, :, nx - LANES : nx], 64, 1)
        before = pltpu.roll(far_left, 125 - 8 * f, 1)
        after = pltpu.roll(far_right, 64 - 8 * f, 1)
        tile = jnp.where(lane < 32, begin, end)
        tile = jnp.where(lane >= 125, before, tile)
        seam.append(jnp.where((lane >= 64) & (lane < 67), after, tile))
    profiles = primitives(seam)
    up, down = shifts(LANES, 1)
    for f, difference in enumerate(flux_differences(profiles, up, down, 1)):
        df[f, :, 0:LANES] = jnp.where(lane < 3, difference, df[f, :, 0:LANES])
        df[f, :, nx - LANES : nx] = jnp.where(
            lane >= 125, pltpu.roll(difference, 64, 1), df[f, :, nx - LANES : nx]
        )

    pltpu.make_async_copy(others, others, peak_recv).wait()
    peak = jnp.maximum(mine[...], jnp.max(others[...], axis=0))
    half_step = (0.5 * COURANT) / peak

    up, down = shifts(total, 0)

    wide = 2 * LANES if nx % (2 * LANES) == 0 else LANES
    half_step = jnp.concatenate([half_step] * (wide // LANES), axis=1)

    @pl.loop(0, nx // wide)
    def _(chunk):
        at = pl.ds(pl.multiple_of(chunk * wide, wide), wide)
        cells = [u[f, :, at] - half_step * df[f, :, at] for f in range(5)]
        profiles = primitives(cells)
        for f, difference in enumerate(flux_differences(profiles, up, down, 2)):
            result = cells[f] - half_step * difference
            out[f, 0, :, at] = result[0:ny]

    for copy in halos:
        copy.wait_send()
    pltpu.make_async_copy(others, others, peak_send).wait()


def local(rows, cols, fields):
    ny, nx = fields.shape[2], fields.shape[3]
    vmem = lambda *shape: pltpu.VMEM(shape, jnp.float32)
    dma = pltpu.SemaphoreType.DMA
    return pl.pallas_call(
        functools.partial(kernel, rows, cols),
        out_shape=jax.ShapeDtypeStruct(fields.shape, fields.dtype),
        in_specs=[pl.BlockSpec(memory_space=pltpu.HBM)],
        out_specs=pl.BlockSpec(memory_space=pltpu.VMEM),
        scratch_shapes=[
            vmem(5, ny + SUBLANES, nx),
            vmem(5, ny + SUBLANES, nx),
            vmem(ny, LANES),
            vmem(ny, LANES),
            vmem(16, nx),
            vmem(16, nx),
            vmem(ny, LANES),
            vmem(ny, LANES),
            vmem(16, nx),
            vmem(16, nx),
            vmem(4, SUBLANES, LANES),
            vmem(1, LANES),
            vmem(rows * cols - 1, 1, LANES),
            dma,
            dma((8,)),
            dma((8,)),
            dma,
            dma,
        ],
        compiler_params=pltpu.CompilerParams(
            collective_id=0, has_side_effects=True, vmem_limit_bytes=55072 * 1024
        ),
        name="sweeps",
    )(fields)


def solution(mesh):
    spec = P(None, None, "col", "row")
    return jax.shard_map(
        functools.partial(local, mesh.shape["row"], mesh.shape["col"]),
        mesh=mesh,
        in_specs=(spec,),
        out_specs=spec,
        check_vma=False,
    )
```

```python
import functools

import jax
import jax.numpy as jnp
from jax import lax
from jax.experimental import pallas as pl
from jax.experimental.pallas import tpu as pltpu
from jax.sharding import PartitionSpec as P

GAMMA = 1.4
COURANT = 0.3
MESH = pl.DeviceIdType.MESH
LANES = 128
SUBLANES = 8
TINY = 1e-37
UNROLLED = 64


def sound(density, pressure):
    scaled = GAMMA * pressure
    return scaled * lax.rsqrt(jnp.maximum(scaled, TINY)) * lax.rsqrt(density)


def primitives(cells):
    density = cells[0]
    inverse_density = pl.reciprocal(density, approx=True)
    velocity = [cells[k] * inverse_density for k in (1, 2, 3)]
    square = velocity[0] * velocity[0] + velocity[1] * velocity[1] + velocity[2] * velocity[2]
    pressure = (GAMMA - 1.0) * (cells[4] - 0.5 * density * square)
    return [density] + velocity + [pressure]


def limited(first, second):
    return jnp.minimum(jnp.maximum(first, jnp.minimum(second, 0.0)), jnp.maximum(second, 0.0))


def face_values(q, up, down):
    after = up(q)
    jump = after - q
    rise = 0.5 * jump + (1.0 / 12.0) * (down(jump) - up(jump))
    rise = jnp.minimum(jnp.maximum(rise, jnp.minimum(jump, 0.0)), jnp.maximum(jump, 0.0))
    next_fall = jump - rise
    fall, next_rise = down(next_fall), up(rise)
    right = q + limited(rise, fall + fall)
    next_left = after - limited(next_fall, next_rise + next_rise)
    return right, next_left


def flux_differences(profiles, up, down, normal):
    pairs = [face_values(q, up, down) for q in profiles]
    sides = [[pair[side] for pair in pairs] for side in range(2)]
    signal = None
    for density, pressure, speed in [(side[0], side[4], side[normal]) for side in sides]:
        own = jnp.abs(speed) + sound(density, pressure)
        signal = own if signal is None else jnp.maximum(signal, own)
    shifted = [sides[0][normal] + signal, sides[1][normal] - signal]
    mass = [side[0] * speed for side, speed in zip(sides, shifted)]
    fluxes = [mass[0] + mass[1]]
    kinetic = None
    for k in (1, 2, 3):
        left, right = mass[0] * sides[0][k], mass[1] * sides[1][k]
        work = left * sides[0][k] + right * sides[1][k]
        kinetic = work if kinetic is None else kinetic + work
        fluxes.append(left + right)
    fluxes[normal] = fluxes[normal] + (sides[0][4] + sides[1][4])
    energy = 0.5 * kinetic
    for side, speed in zip(sides, shifted):
        energy = energy + side[4] * (speed * (1.0 / (GAMMA - 1.0)) + side[normal])
    fluxes.append(energy)
    return [flux - down(flux) for flux in fluxes]


def shifts(length, axis):
    return (
        lambda a: pltpu.roll(a, length - 1, axis),
        lambda a: pltpu.roll(a, 1, axis),
    )


def kernel(
    rows, cols, x, out, u, df, xr, xl, yt, yb, rxl, rxr, rya, ryb, rc, mine, others,
    in_sem, halo_send, halo_recv, peak_send, peak_recv,
):
    ny, nx = x.shape[2], x.shape[3]
    me_r, me_c = lax.axis_index("row"), lax.axis_index("col")

    def row_at(step):
        return lax.rem(me_r + (step % rows), rows)

    def col_at(step):
        return lax.rem(me_c + (step % cols), cols)

    load = pltpu.make_async_copy(x.at[:, 0], u.at[:, pl.ds(0, ny)], in_sem)
    load.start()

    barrier = pltpu.get_barrier_semaphore()
    count = rows * cols

    def for_peers(act):
        if count <= UNROLLED:
            at_row = [row_at(a) for a in range(rows)]
            at_col = [col_at(b) for b in range(cols)]
            for d in range(1, count):
                act(d, (at_row[d // cols], at_col[d % cols]))
        else:

            @pl.loop(1, count)
            def _(d):
                act(d, (lax.rem(me_r + d // cols, rows), lax.rem(me_c + d % cols, cols)))

    def greet(d, peer):
        pl.semaphore_signal(barrier, inc=1, device_id=peer, device_id_type=MESH)

    for_peers(greet)
    load.wait()

    peak = None
    for r in range(0, ny, SUBLANES):
        profiles = primitives([u[f, r : r + SUBLANES, :] for f in range(5)])
        speed = jnp.maximum(jnp.abs(profiles[1]), jnp.abs(profiles[2]))
        speed = speed + sound(profiles[0], profiles[4])
        for c in range(0, nx, LANES):
            part = speed[:, c : c + LANES]
            peak = part if peak is None else jnp.maximum(peak, part)
    peak = jnp.max(jnp.max(peak, axis=0, keepdims=True), axis=1, keepdims=True)
    mine[...] = jnp.broadcast_to(peak, mine.shape)

    lane = lax.broadcasted_iota(jnp.int32, (ny, LANES), 1)
    pack_r = pack_l = None
    for f in range(5):
        edge_r = pltpu.roll(u[f, 0:ny, nx - LANES : nx], 8 * f + 3, 1)
        edge_l = u[f, 0:ny, 0:LANES]
        if f:
            edge_l = pltpu.roll(edge_l, 8 * f, 1)
            pack_r = jnp.where(lane < 8 * f, pack_r, edge_r)
            pack_l = jnp.where(lane < 8 * f, pack_l, edge_l)
        else:
            pack_r, pack_l = edge_r, edge_l
    xr[...] = pack_r
    xl[...] = pack_l
    for f in range(5):
        yt[3 * f : 3 * f + 3, :] = u[f, 0:3, :]
        yb[3 * f : 3 * f + 3, :] = u[f, ny - 3 : ny, :]
    yt[15:16, :] = u[0, 0:1, :]
    yb[15:16, :] = u[0, 0:1, :]
    pl.semaphore_wait(barrier, count - 1)

    def tell(d, peer):
        pltpu.make_async_remote_copy(
            src_ref=mine, dst_ref=others.at[d - 1], send_sem=peak_send, recv_sem=peak_recv,
            device_id=peer, device_id_type=MESH,
        ).start()

    for_peers(tell)
    top, bottom = pl.ds(0, SUBLANES), pl.ds(ny - SUBLANES, SUBLANES)
    halos = []
    for i, (src, dst, device) in enumerate(
        [
            (yb, rya, (me_r, col_at(1))),
            (yt, ryb, (me_r, col_at(-1))),
            (xr, rxl, (row_at(1), me_c)),
            (xl, rxr, (row_at(-1), me_c)),
            (xr.at[bottom], rc.at[0], (row_at(1), col_at(1))),
            (xl.at[bottom], rc.at[1], (row_at(-1), col_at(1))),
            (xr.at[top], rc.at[2], (row_at(1), col_at(-1))),
            (xl.at[top], rc.at[3], (row_at(-1), col_at(-1))),
        ]
    ):
        halos.append(
            pltpu.make_async_remote_copy(
                src_ref=src, dst_ref=dst, send_sem=halo_send.at[i], recv_sem=halo_recv.at[i],
                device_id=device, device_id_type=MESH,
            )
        )
        halos[i].start()

    up, down = shifts(nx, 1)

    def sweep_tile(at):
        profiles = primitives([u[f, at, :] for f in range(5)])
        for f, difference in enumerate(flux_differences(profiles, up, down, 1)):
            df[f, at, :] = difference

    deep = 2 * SUBLANES if ny % (2 * SUBLANES) == 0 else SUBLANES

    @pl.loop(0, ny // deep)
    def _(tile):
        sweep_tile(pl.ds(pl.multiple_of(tile * deep, deep), deep))

    halos[0].wait_recv()
    halos[1].wait_recv()
    for f in range(5):
        u[f, ny : ny + 3, :] = ryb[3 * f : 3 * f + 3, :]
        u[f, ny + 3 : ny + 5, :] = u[f, 3:5, :]
        u[f, ny + 5 : ny + 8, :] = rya[3 * f : 3 * f + 3, :]
    sweep_tile(pl.ds(ny, SUBLANES))

    for copy in halos[2:]:
        copy.wait_recv()
    total = ny + SUBLANES
    lane = lax.broadcasted_iota(jnp.int32, (total, LANES), 1)
    below = lax.broadcasted_iota(jnp.int32, (SUBLANES, LANES), 0) < 4
    far_left = jnp.concatenate([rxl[...], jnp.where(below, rc[2], rc[0])], axis=0)
    far_right = jnp.concatenate([rxr[...], jnp.where(below, rc[3], rc[1])], axis=0)
    seam = []
    for f in range(5):
        begin = u[f, :, 0:LANES]
        end = pltpu.roll(u[f, :, nx - LANES : nx], 64, 1)
        before = pltpu.roll(far_left, 125 - 8 * f, 1)
        after = pltpu.roll(far_right, 64 - 8 * f, 1)
        tile = jnp.where(lane < 32, begin, end)
        tile = jnp.where(lane >= 125, before, tile)
        seam.append(jnp.where((lane >= 64) & (lane < 67), after, tile))
    profiles = primitives(seam)
    up, down = shifts(LANES, 1)
    for f, difference in enumerate(flux_differences(profiles, up, down, 1)):
        df[f, :, 0:LANES] = jnp.where(lane < 3, difference, df[f, :, 0:LANES])
        df[f, :, nx - LANES : nx] = jnp.where(
            lane >= 125, pltpu.roll(difference, 64, 1), df[f, :, nx - LANES : nx]
        )

    pltpu.make_async_copy(others, others, peak_recv).wait()
    peak = jnp.maximum(mine[...], jnp.max(others[...], axis=0))
    half_step = (0.5 * COURANT) / peak

    up, down = shifts(total, 0)

    wide = 2 * LANES if nx % (2 * LANES) == 0 else LANES
    half_step = jnp.concatenate([half_step] * (wide // LANES), axis=1)

    for begin in range(0, nx, wide):
        at = pl.ds(begin, wide)
        cells = [u[f, :, at] - half_step * df[f, :, at] for f in range(5)]
        profiles = primitives(cells)
        for f, difference in enumerate(flux_differences(profiles, up, down, 2)):
            result = cells[f] - half_step * difference
            out[f, 0, :, at] = result[0:ny]

    for copy in halos:
        copy.wait_send()
    pltpu.make_async_copy(others, others, peak_send).wait()


def local(rows, cols, fields):
    ny, nx = fields.shape[2], fields.shape[3]
    vmem = lambda *shape: pltpu.VMEM(shape, jnp.float32)
    dma = pltpu.SemaphoreType.DMA
    return pl.pallas_call(
        functools.partial(kernel, rows, cols),
        out_shape=jax.ShapeDtypeStruct(fields.shape, fields.dtype),
        in_specs=[pl.BlockSpec(memory_space=pltpu.HBM)],
        out_specs=pl.BlockSpec(memory_space=pltpu.VMEM),
        scratch_shapes=[
            vmem(5, ny + SUBLANES, nx),
            vmem(5, ny + SUBLANES, nx),
            vmem(ny, LANES),
            vmem(ny, LANES),
            vmem(16, nx),
            vmem(16, nx),
            vmem(ny, LANES),
            vmem(ny, LANES),
            vmem(16, nx),
            vmem(16, nx),
            vmem(4, SUBLANES, LANES),
            vmem(1, LANES),
            vmem(rows * cols - 1, 1, LANES),
            dma,
            dma((8,)),
            dma((8,)),
            dma,
            dma,
        ],
        compiler_params=pltpu.CompilerParams(
            collective_id=0, has_side_effects=True, vmem_limit_bytes=55072 * 1024
        ),
        name="sweeps",
    )(fields)


def solution(mesh):
    spec = P(None, None, "col", "row")
    return jax.shard_map(
        functools.partial(local, mesh.shape["row"], mesh.shape["col"]),
        mesh=mesh,
        in_specs=(spec,),
        out_specs=spec,
        check_vma=False,
    )
```

```python
import functools

import jax
import jax.numpy as jnp
from jax import lax
from jax.experimental import pallas as pl
from jax.experimental.pallas import tpu as pltpu
from jax.sharding import PartitionSpec as P

GAMMA = 1.4
COURANT = 0.3
MESH = pl.DeviceIdType.MESH
LANES = 128
SUBLANES = 8
TINY = 1e-37
UNROLLED = 64


def sound(density, pressure):
    scaled = GAMMA * pressure
    return scaled * lax.rsqrt(jnp.maximum(scaled, TINY)) * lax.rsqrt(density)


def primitives(cells):
    density = cells[0]
    inverse_density = pl.reciprocal(density, approx=True)
    velocity = [cells[k] * inverse_density for k in (1, 2, 3)]
    square = velocity[0] * velocity[0] + velocity[1] * velocity[1] + velocity[2] * velocity[2]
    pressure = (GAMMA - 1.0) * (cells[4] - 0.5 * density * square)
    return [density] + velocity + [pressure]


def limited(first, second):
    return jnp.minimum(jnp.maximum(first, jnp.minimum(second, 0.0)), jnp.maximum(second, 0.0))


def face_values(q, up, down):
    after = up(q)
    jump = after - q
    rise = 0.5 * jump + (1.0 / 12.0) * (down(jump) - up(jump))
    rise = jnp.minimum(jnp.maximum(rise, jnp.minimum(jump, 0.0)), jnp.maximum(jump, 0.0))
    next_fall = jump - rise
    fall, next_rise = down(next_fall), up(rise)
    right = q + limited(rise, fall + fall)
    next_left = after - limited(next_fall, next_rise + next_rise)
    return right, next_left


def flux_differences(profiles, up, down, normal):
    pairs = [face_values(q, up, down) for q in profiles]
    sides = [[pair[side] for pair in pairs] for side in range(2)]
    signal = None
    for density, pressure, speed in [(side[0], side[4], side[normal]) for side in sides]:
        own = jnp.abs(speed) + sound(density, pressure)
        signal = own if signal is None else jnp.maximum(signal, own)
    shifted = [sides[0][normal] + signal, sides[1][normal] - signal]
    mass = [side[0] * speed for side, speed in zip(sides, shifted)]
    fluxes = [mass[0] + mass[1]]
    kinetic = None
    for k in (1, 2, 3):
        left, right = mass[0] * sides[0][k], mass[1] * sides[1][k]
        work = left * sides[0][k] + right * sides[1][k]
        kinetic = work if kinetic is None else kinetic + work
        fluxes.append(left + right)
    fluxes[normal] = fluxes[normal] + (sides[0][4] + sides[1][4])
    energy = 0.5 * kinetic
    for side, speed in zip(sides, shifted):
        energy = energy + side[4] * (speed * (1.0 / (GAMMA - 1.0)) + side[normal])
    fluxes.append(energy)
    return [flux - down(flux) for flux in fluxes]


def shifts(length, axis):
    return (
        lambda a: pltpu.roll(a, length - 1, axis),
        lambda a: pltpu.roll(a, 1, axis),
    )


def kernel(
    rows, cols, x, out, u, df, xr, xl, yt, yb, rxl, rxr, rya, ryb, rc, mine, others,
    in_sem, halo_send, halo_recv, peak_send, peak_recv,
):
    ny, nx = x.shape[2], x.shape[3]
    me_r, me_c = lax.axis_index("row"), lax.axis_index("col")

    def row_at(step):
        return lax.rem(me_r + (step % rows), rows)

    def col_at(step):
        return lax.rem(me_c + (step % cols), cols)

    load = pltpu.make_async_copy(x.at[:, 0], u.at[:, pl.ds(0, ny)], in_sem)
    load.start()

    barrier = pltpu.get_barrier_semaphore()
    count = rows * cols

    def for_peers(act):
        if count <= UNROLLED:
            at_row = [row_at(a) for a in range(rows)]
            at_col = [col_at(b) for b in range(cols)]
            for d in range(1, count):
                act(d, (at_row[d // cols], at_col[d % cols]))
        else:

            @pl.loop(1, count)
            def _(d):
                act(d, (lax.rem(me_r + d // cols, rows), lax.rem(me_c + d % cols, cols)))

    def greet(d, peer):
        pl.semaphore_signal(barrier, inc=1, device_id=peer, device_id_type=MESH)

    for_peers(greet)
    load.wait()

    peak = None
    for r in range(0, ny, SUBLANES):
        profiles = primitives([u[f, r : r + SUBLANES, :] for f in range(5)])
        speed = jnp.maximum(jnp.abs(profiles[1]), jnp.abs(profiles[2]))
        speed = speed + sound(profiles[0], profiles[4])
        for c in range(0, nx, LANES):
            part = speed[:, c : c + LANES]
            peak = part if peak is None else jnp.maximum(peak, part)
    peak = jnp.max(jnp.max(peak, axis=0, keepdims=True), axis=1, keepdims=True)
    mine[...] = jnp.broadcast_to(peak, mine.shape)

    lane = lax.broadcasted_iota(jnp.int32, (ny, LANES), 1)
    pack_r = pack_l = None
    for f in range(5):
        edge_r = pltpu.roll(u[f, 0:ny, nx - LANES : nx], 8 * f + 3, 1)
        edge_l = u[f, 0:ny, 0:LANES]
        if f:
            edge_l = pltpu.roll(edge_l, 8 * f, 1)
            pack_r = jnp.where(lane < 8 * f, pack_r, edge_r)
            pack_l = jnp.where(lane < 8 * f, pack_l, edge_l)
        else:
            pack_r, pack_l = edge_r, edge_l
    xr[...] = pack_r
    xl[...] = pack_l
    for f in range(5):
        yt[3 * f : 3 * f + 3, :] = u[f, 0:3, :]
        yb[3 * f : 3 * f + 3, :] = u[f, ny - 3 : ny, :]
    yt[15:16, :] = u[0, 0:1, :]
    yb[15:16, :] = u[0, 0:1, :]
    pl.semaphore_wait(barrier, count - 1)

    def tell(d, peer):
        pltpu.make_async_remote_copy(
            src_ref=mine, dst_ref=others.at[d - 1], send_sem=peak_send, recv_sem=peak_recv,
            device_id=peer, device_id_type=MESH,
        ).start()

    top, bottom = pl.ds(0, SUBLANES), pl.ds(ny - SUBLANES, SUBLANES)
    halos = []
    for i, (src, dst, device) in enumerate(
        [
            (yb, rya, (me_r, col_at(1))),
            (yt, ryb, (me_r, col_at(-1))),
            (xr, rxl, (row_at(1), me_c)),
            (xl, rxr, (row_at(-1), me_c)),
            (xr.at[bottom], rc.at[0], (row_at(1), col_at(1))),
            (xl.at[bottom], rc.at[1], (row_at(-1), col_at(1))),
            (xr.at[top], rc.at[2], (row_at(1), col_at(-1))),
            (xl.at[top], rc.at[3], (row_at(-1), col_at(-1))),
        ]
    ):
        halos.append(
            pltpu.make_async_remote_copy(
                src_ref=src, dst_ref=dst, send_sem=halo_send.at[i], recv_sem=halo_recv.at[i],
                device_id=device, device_id_type=MESH,
            )
        )

    first, last = me_c == 0, me_c == cols - 1
    downward, upward = (halos[0], halos[4], halos[5]), (halos[1], halos[6], halos[7])

    def start_when(condition, copies):
        @pl.when(condition)
        def _():
            for copy in copies:
                copy.start()

    start_when(last, downward)
    start_when(first, upward)
    for_peers(tell)
    start_when(jnp.logical_not(last), downward)
    start_when(jnp.logical_not(first), upward)
    halos[2].start()
    halos[3].start()

    up, down = shifts(nx, 1)

    def sweep_tile(at):
        profiles = primitives([u[f, at, :] for f in range(5)])
        for f, difference in enumerate(flux_differences(profiles, up, down, 1)):
            df[f, at, :] = difference

    deep = 2 * SUBLANES if ny % (2 * SUBLANES) == 0 else SUBLANES

    @pl.loop(0, ny // deep)
    def _(tile):
        sweep_tile(pl.ds(pl.multiple_of(tile * deep, deep), deep))

    halos[0].wait_recv()
    halos[1].wait_recv()
    for f in range(5):
        u[f, ny : ny + 3, :] = ryb[3 * f : 3 * f + 3, :]
        u[f, ny + 3 : ny + 5, :] = u[f, 3:5, :]
        u[f, ny + 5 : ny + 8, :] = rya[3 * f : 3 * f + 3, :]
    sweep_tile(pl.ds(ny, SUBLANES))

    for copy in halos[2:]:
        copy.wait_recv()
    total = ny + SUBLANES
    lane = lax.broadcasted_iota(jnp.int32, (total, LANES), 1)
    below = lax.broadcasted_iota(jnp.int32, (SUBLANES, LANES), 0) < 4
    far_left = jnp.concatenate([rxl[...], jnp.where(below, rc[2], rc[0])], axis=0)
    far_right = jnp.concatenate([rxr[...], jnp.where(below, rc[3], rc[1])], axis=0)
    seam = []
    for f in range(5):
        begin = u[f, :, 0:LANES]
        end = pltpu.roll(u[f, :, nx - LANES : nx], 64, 1)
        before = pltpu.roll(far_left, 125 - 8 * f, 1)
        after = pltpu.roll(far_right, 64 - 8 * f, 1)
        tile = jnp.where(lane < 32, begin, end)
        tile = jnp.where(lane >= 125, before, tile)
        seam.append(jnp.where((lane >= 64) & (lane < 67), after, tile))
    profiles = primitives(seam)
    up, down = shifts(LANES, 1)
    for f, difference in enumerate(flux_differences(profiles, up, down, 1)):
        df[f, :, 0:LANES] = jnp.where(lane < 3, difference, df[f, :, 0:LANES])
        df[f, :, nx - LANES : nx] = jnp.where(
            lane >= 125, pltpu.roll(difference, 64, 1), df[f, :, nx - LANES : nx]
        )

    pltpu.make_async_copy(others, others, peak_recv).wait()
    peak = jnp.maximum(mine[...], jnp.max(others[...], axis=0))
    half_step = (0.5 * COURANT) / peak

    up, down = shifts(total, 0)

    wide = 2 * LANES if nx % (2 * LANES) == 0 else LANES
    half_step = jnp.concatenate([half_step] * (wide // LANES), axis=1)

    for begin in range(0, nx, wide):
        at = pl.ds(begin, wide)
        cells = [u[f, :, at] - half_step * df[f, :, at] for f in range(5)]
        profiles = primitives(cells)
        for f, difference in enumerate(flux_differences(profiles, up, down, 2)):
            result = cells[f] - half_step * difference
            out[f, 0, :, at] = result[0:ny]

    for copy in halos:
        copy.wait_send()
    pltpu.make_async_copy(others, others, peak_send).wait()


def local(rows, cols, fields):
    ny, nx = fields.shape[2], fields.shape[3]
    vmem = lambda *shape: pltpu.VMEM(shape, jnp.float32)
    dma = pltpu.SemaphoreType.DMA
    return pl.pallas_call(
        functools.partial(kernel, rows, cols),
        out_shape=jax.ShapeDtypeStruct(fields.shape, fields.dtype),
        in_specs=[pl.BlockSpec(memory_space=pltpu.HBM)],
        out_specs=pl.BlockSpec(memory_space=pltpu.VMEM),
        scratch_shapes=[
            vmem(5, ny + SUBLANES, nx),
            vmem(5, ny + SUBLANES, nx),
            vmem(ny, LANES),
            vmem(ny, LANES),
            vmem(16, nx),
            vmem(16, nx),
            vmem(ny, LANES),
            vmem(ny, LANES),
            vmem(16, nx),
            vmem(16, nx),
            vmem(4, SUBLANES, LANES),
            vmem(1, LANES),
            vmem(rows * cols - 1, 1, LANES),
            dma,
            dma((8,)),
            dma((8,)),
            dma,
            dma,
        ],
        compiler_params=pltpu.CompilerParams(
            collective_id=0, has_side_effects=True, vmem_limit_bytes=55072 * 1024
        ),
        name="sweeps",
    )(fields)


def solution(mesh):
    spec = P(None, None, "col", "row")
    return jax.shard_map(
        functools.partial(local, mesh.shape["row"], mesh.shape["col"]),
        mesh=mesh,
        in_specs=(spec,),
        out_specs=spec,
        check_vma=False,
    )
```

```python
import functools

import jax
import jax.numpy as jnp
from jax import lax
from jax.experimental import pallas as pl
from jax.experimental.pallas import tpu as pltpu
from jax.sharding import PartitionSpec as P

GAMMA = 1.4
COURANT = 0.3
MESH = pl.DeviceIdType.MESH
LANES = 128
SUBLANES = 8
TINY = 1e-37
UNROLLED = 64


def sound(density, pressure):
    scaled = GAMMA * pressure
    return scaled * lax.rsqrt(jnp.maximum(scaled, TINY)) * lax.rsqrt(density)


def primitives(cells):
    density = cells[0]
    inverse_density = pl.reciprocal(density, approx=True)
    velocity = [cells[k] * inverse_density for k in (1, 2, 3)]
    square = velocity[0] * velocity[0] + velocity[1] * velocity[1] + velocity[2] * velocity[2]
    pressure = (GAMMA - 1.0) * (cells[4] - 0.5 * density * square)
    return [density] + velocity + [pressure]


def limited(first, second):
    return jnp.minimum(jnp.maximum(first, jnp.minimum(second, 0.0)), jnp.maximum(second, 0.0))


def face_values(q, up, down):
    after = up(q)
    jump = after - q
    rise = 0.5 * jump + (1.0 / 12.0) * (down(jump) - up(jump))
    rise = jnp.minimum(jnp.maximum(rise, jnp.minimum(jump, 0.0)), jnp.maximum(jump, 0.0))
    next_fall = jump - rise
    fall, next_rise = down(next_fall), up(rise)
    right = q + limited(rise, fall + fall)
    next_left = after - limited(next_fall, next_rise + next_rise)
    return right, next_left


def flux_differences(profiles, up, down, normal):
    pairs = [face_values(q, up, down) for q in profiles]
    sides = [[pair[side] for pair in pairs] for side in range(2)]
    signal = None
    for density, pressure, speed in [(side[0], side[4], side[normal]) for side in sides]:
        own = jnp.abs(speed) + sound(density, pressure)
        signal = own if signal is None else jnp.maximum(signal, own)
    shifted = [sides[0][normal] + signal, sides[1][normal] - signal]
    mass = [side[0] * speed for side, speed in zip(sides, shifted)]
    fluxes = [mass[0] + mass[1]]
    kinetic = None
    for k in (1, 2, 3):
        left, right = mass[0] * sides[0][k], mass[1] * sides[1][k]
        work = left * sides[0][k] + right * sides[1][k]
        kinetic = work if kinetic is None else kinetic + work
        fluxes.append(left + right)
    fluxes[normal] = fluxes[normal] + (sides[0][4] + sides[1][4])
    energy = 0.5 * kinetic
    for side, speed in zip(sides, shifted):
        energy = energy + side[4] * (speed * (1.0 / (GAMMA - 1.0)) + side[normal])
    fluxes.append(energy)
    return [flux - down(flux) for flux in fluxes]


def shifts(length, axis):
    return (
        lambda a: pltpu.roll(a, length - 1, axis),
        lambda a: pltpu.roll(a, 1, axis),
    )


def kernel(
    rows, cols, x, out, u, df, xr, xl, yt, yb, rxl, rxr, rya, ryb, rc, mine, theirs, both, others,
    in_sem, halo_send, halo_recv, pair_send, pair_recv, peak_send, peak_recv,
):
    ny, nx = x.shape[2], x.shape[3]
    me_r, me_c = lax.axis_index("row"), lax.axis_index("col")

    def row_at(step):
        return lax.rem(me_r + (step % rows), rows)

    def col_at(step):
        return lax.rem(me_c + (step % cols), cols)

    load = pltpu.make_async_copy(x.at[:, 0], u.at[:, pl.ds(0, ny)], in_sem)
    load.start()

    barrier = pltpu.get_barrier_semaphore()
    partner = (me_r, me_c + 1 - 2 * lax.rem(me_c, 2))
    half = cols // 2
    count = rows * half

    def for_chips(act):
        if count <= UNROLLED:
            at_row = [row_at(a) for a in range(rows)]
            at_col = [col_at(2 * b) for b in range(half)]
            for d in range(1, count):
                act(d, (at_row[d // half], at_col[d % half]))
        else:

            @pl.loop(1, count)
            def _(d):
                step = 2 * (d % half)
                act(d, (lax.rem(me_r + d // half, rows), lax.rem(me_c + step, cols)))

    def greet(d, peer):
        pl.semaphore_signal(barrier, inc=1, device_id=peer, device_id_type=MESH)

    near = [(me_r, col_at(b)) for b in (1, -1)]
    near += [(row_at(a), col_at(b)) for a in (1, -1) for b in (1, -1)]
    for peer in near:
        greet(0, peer)
    for_chips(greet)
    load.wait()

    peak = None
    for r in range(0, ny, SUBLANES):
        profiles = primitives([u[f, r : r + SUBLANES, :] for f in range(5)])
        speed = jnp.maximum(jnp.abs(profiles[1]), jnp.abs(profiles[2]))
        speed = speed + sound(profiles[0], profiles[4])
        for c in range(0, nx, LANES):
            part = speed[:, c : c + LANES]
            peak = part if peak is None else jnp.maximum(peak, part)
    peak = jnp.max(jnp.max(peak, axis=0, keepdims=True), axis=1, keepdims=True)
    mine[...] = jnp.broadcast_to(peak, mine.shape)

    lane = lax.broadcasted_iota(jnp.int32, (ny, LANES), 1)
    pack_r = pack_l = None
    for f in range(5):
        edge_r = pltpu.roll(u[f, 0:ny, nx - LANES : nx], 8 * f + 3, 1)
        edge_l = u[f, 0:ny, 0:LANES]
        if f:
            edge_l = pltpu.roll(edge_l, 8 * f, 1)
            pack_r = jnp.where(lane < 8 * f, pack_r, edge_r)
            pack_l = jnp.where(lane < 8 * f, pack_l, edge_l)
        else:
            pack_r, pack_l = edge_r, edge_l
    xr[...] = pack_r
    xl[...] = pack_l
    for f in range(5):
        yt[3 * f : 3 * f + 3, :] = u[f, 0:3, :]
        yb[3 * f : 3 * f + 3, :] = u[f, ny - 3 : ny, :]
    yt[15:16, :] = u[0, 0:1, :]
    yb[15:16, :] = u[0, 0:1, :]
    pl.semaphore_wait(barrier, count - 1 + len(near))
    pair = pltpu.make_async_remote_copy(
        src_ref=mine, dst_ref=theirs, send_sem=pair_send, recv_sem=pair_recv,
        device_id=partner, device_id_type=MESH,
    )
    pair.start()
    pair.wait_recv()
    both[...] = jnp.maximum(mine[...], theirs[...])

    def tell(d, peer):
        pltpu.make_async_remote_copy(
            src_ref=both, dst_ref=others.at[d - 1], send_sem=peak_send, recv_sem=peak_recv,
            device_id=peer, device_id_type=MESH,
        ).start()

    for_chips(tell)

    top, bottom = pl.ds(0, SUBLANES), pl.ds(ny - SUBLANES, SUBLANES)
    halos = []
    for i, (src, dst, device) in enumerate(
        [
            (yb, rya, (me_r, col_at(1))),
            (yt, ryb, (me_r, col_at(-1))),
            (xr, rxl, (row_at(1), me_c)),
            (xl, rxr, (row_at(-1), me_c)),
            (xr.at[bottom], rc.at[0], (row_at(1), col_at(1))),
            (xl.at[bottom], rc.at[1], (row_at(-1), col_at(1))),
            (xr.at[top], rc.at[2], (row_at(1), col_at(-1))),
            (xl.at[top], rc.at[3], (row_at(-1), col_at(-1))),
        ]
    ):
        halos.append(
            pltpu.make_async_remote_copy(
                src_ref=src, dst_ref=dst, send_sem=halo_send.at[i], recv_sem=halo_recv.at[i],
                device_id=device, device_id_type=MESH,
            )
        )
        halos[i].start()

    up, down = shifts(nx, 1)

    def sweep_tile(at):
        profiles = primitives([u[f, at, :] for f in range(5)])
        for f, difference in enumerate(flux_differences(profiles, up, down, 1)):
            df[f, at, :] = difference

    deep = 2 * SUBLANES if ny % (2 * SUBLANES) == 0 else SUBLANES

    @pl.loop(0, ny // deep)
    def _(tile):
        sweep_tile(pl.ds(pl.multiple_of(tile * deep, deep), deep))

    halos[0].wait_recv()
    halos[1].wait_recv()
    for f in range(5):
        u[f, ny : ny + 3, :] = ryb[3 * f : 3 * f + 3, :]
        u[f, ny + 3 : ny + 5, :] = u[f, 3:5, :]
        u[f, ny + 5 : ny + 8, :] = rya[3 * f : 3 * f + 3, :]
    sweep_tile(pl.ds(ny, SUBLANES))

    for copy in halos[2:]:
        copy.wait_recv()
    total = ny + SUBLANES
    lane = lax.broadcasted_iota(jnp.int32, (total, LANES), 1)
    below = lax.broadcasted_iota(jnp.int32, (SUBLANES, LANES), 0) < 4
    far_left = jnp.concatenate([rxl[...], jnp.where(below, rc[2], rc[0])], axis=0)
    far_right = jnp.concatenate([rxr[...], jnp.where(below, rc[3], rc[1])], axis=0)
    seam = []
    for f in range(5):
        begin = u[f, :, 0:LANES]
        end = pltpu.roll(u[f, :, nx - LANES : nx], 64, 1)
        before = pltpu.roll(far_left, 125 - 8 * f, 1)
        after = pltpu.roll(far_right, 64 - 8 * f, 1)
        tile = jnp.where(lane < 32, begin, end)
        tile = jnp.where(lane >= 125, before, tile)
        seam.append(jnp.where((lane >= 64) & (lane < 67), after, tile))
    profiles = primitives(seam)
    up, down = shifts(LANES, 1)
    for f, difference in enumerate(flux_differences(profiles, up, down, 1)):
        df[f, :, 0:LANES] = jnp.where(lane < 3, difference, df[f, :, 0:LANES])
        df[f, :, nx - LANES : nx] = jnp.where(
            lane >= 125, pltpu.roll(difference, 64, 1), df[f, :, nx - LANES : nx]
        )

    pltpu.make_async_copy(others, others, peak_recv).wait()
    peak = jnp.maximum(both[...], jnp.max(others[...], axis=0))
    half_step = (0.5 * COURANT) / peak

    up, down = shifts(total, 0)

    wide = 2 * LANES if nx % (2 * LANES) == 0 else LANES
    half_step = jnp.concatenate([half_step] * (wide // LANES), axis=1)

    @pl.loop(0, nx // wide)
    def _(chunk):
        at = pl.ds(pl.multiple_of(chunk * wide, wide), wide)
        cells = [u[f, :, at] - half_step * df[f, :, at] for f in range(5)]
        profiles = primitives(cells)
        for f, difference in enumerate(flux_differences(profiles, up, down, 2)):
            result = cells[f] - half_step * difference
            out[f, 0, :, at] = result[0:ny]

    for copy in halos:
        copy.wait_send()
    pair.wait_send()
    pltpu.make_async_copy(others, others, peak_send).wait()


def local(rows, cols, fields):
    ny, nx = fields.shape[2], fields.shape[3]
    vmem = lambda *shape: pltpu.VMEM(shape, jnp.float32)
    dma = pltpu.SemaphoreType.DMA
    return pl.pallas_call(
        functools.partial(kernel, rows, cols),
        out_shape=jax.ShapeDtypeStruct(fields.shape, fields.dtype),
        in_specs=[pl.BlockSpec(memory_space=pltpu.HBM)],
        out_specs=pl.BlockSpec(memory_space=pltpu.VMEM),
        scratch_shapes=[
            vmem(5, ny + SUBLANES, nx),
            vmem(5, ny + SUBLANES, nx),
            vmem(ny, LANES),
            vmem(ny, LANES),
            vmem(16, nx),
            vmem(16, nx),
            vmem(ny, LANES),
            vmem(ny, LANES),
            vmem(16, nx),
            vmem(16, nx),
            vmem(4, SUBLANES, LANES),
            vmem(1, LANES),
            vmem(1, LANES),
            vmem(1, LANES),
            vmem(rows * cols // 2 - 1, 1, LANES),
            dma,
            dma((8,)),
            dma((8,)),
            dma,
            dma,
            dma,
            dma,
        ],
        compiler_params=pltpu.CompilerParams(
            collective_id=0, has_side_effects=True, vmem_limit_bytes=55072 * 1024
        ),
        name="sweeps",
    )(fields)


def solution(mesh):
    spec = P(None, None, "col", "row")
    return jax.shard_map(
        functools.partial(local, mesh.shape["row"], mesh.shape["col"]),
        mesh=mesh,
        in_specs=(spec,),
        out_specs=spec,
        check_vma=False,
    )
```

```python
import functools

import jax
import jax.numpy as jnp
from jax import lax
from jax.experimental import pallas as pl
from jax.experimental.pallas import tpu as pltpu
from jax.sharding import PartitionSpec as P

GAMMA = 1.4
COURANT = 0.3
MESH = pl.DeviceIdType.MESH
LANES = 128
SUBLANES = 8
TINY = 1e-37
UNROLLED = 64


def sound(density, pressure):
    scaled = GAMMA * pressure
    return scaled * lax.rsqrt(jnp.maximum(scaled, TINY)) * lax.rsqrt(density)


def primitives(cells):
    density = cells[0]
    inverse_density = pl.reciprocal(density, approx=True)
    velocity = [cells[k] * inverse_density for k in (1, 2, 3)]
    square = velocity[0] * velocity[0] + velocity[1] * velocity[1] + velocity[2] * velocity[2]
    pressure = (GAMMA - 1.0) * (cells[4] - 0.5 * density * square)
    return [density] + velocity + [pressure]


def limited(first, second):
    return jnp.minimum(jnp.maximum(first, jnp.minimum(second, 0.0)), jnp.maximum(second, 0.0))


def face_values(q, up, down):
    after = up(q)
    jump = after - q
    rise = 0.5 * jump + (1.0 / 12.0) * (down(jump) - up(jump))
    rise = jnp.minimum(jnp.maximum(rise, jnp.minimum(jump, 0.0)), jnp.maximum(jump, 0.0))
    next_fall = jump - rise
    fall, next_rise = down(next_fall), up(rise)
    right = q + limited(rise, fall + fall)
    next_left = after - limited(next_fall, next_rise + next_rise)
    return right, next_left


def flux_differences(profiles, up, down, normal):
    pairs = [face_values(q, up, down) for q in profiles]
    sides = [[pair[side] for pair in pairs] for side in range(2)]
    signal = None
    for density, pressure, speed in [(side[0], side[4], side[normal]) for side in sides]:
        own = jnp.abs(speed) + sound(density, pressure)
        signal = own if signal is None else jnp.maximum(signal, own)
    shifted = [sides[0][normal] + signal, sides[1][normal] - signal]
    mass = [side[0] * speed for side, speed in zip(sides, shifted)]
    fluxes = [mass[0] + mass[1]]
    kinetic = None
    for k in (1, 2, 3):
        left, right = mass[0] * sides[0][k], mass[1] * sides[1][k]
        work = left * sides[0][k] + right * sides[1][k]
        kinetic = work if kinetic is None else kinetic + work
        fluxes.append(left + right)
    fluxes[normal] = fluxes[normal] + (sides[0][4] + sides[1][4])
    energy = 0.5 * kinetic
    for side, speed in zip(sides, shifted):
        energy = energy + side[4] * (speed * (1.0 / (GAMMA - 1.0)) + side[normal])
    fluxes.append(energy)
    return [flux - down(flux) for flux in fluxes]


def shifts(length, axis):
    return (
        lambda a: pltpu.roll(a, length - 1, axis),
        lambda a: pltpu.roll(a, 1, axis),
    )


def kernel(
    rows, cols, x, out, u, df, xr, xl, yt, yb, rxl, rxr, rya, ryb, rc, mine, theirs, both, others,
    in_sem, halo_send, halo_recv, pair_send, pair_recv, peak_send, peak_recv,
):
    ny, nx = x.shape[2], x.shape[3]
    me_r, me_c = lax.axis_index("row"), lax.axis_index("col")

    def row_at(step):
        return lax.rem(me_r + (step % rows), rows)

    def col_at(step):
        return lax.rem(me_c + (step % cols), cols)

    load = pltpu.make_async_copy(x.at[:, 0], u.at[:, pl.ds(0, ny)], in_sem)
    load.start()

    barrier = pltpu.get_barrier_semaphore()
    partner = (me_r, me_c + 1 - 2 * lax.rem(me_c, 2))
    half = cols // 2
    count = rows * half

    def for_chips(act):
        if count <= UNROLLED:
            at_row = [row_at(a) for a in range(rows)]
            at_col = [col_at(2 * b) for b in range(half)]
            for d in range(1, count):
                act(d, (at_row[d // half], at_col[d % half]))
        else:

            @pl.loop(1, count)
            def _(d):
                step = 2 * (d % half)
                act(d, (lax.rem(me_r + d // half, rows), lax.rem(me_c + step, cols)))

    def greet(d, peer):
        pl.semaphore_signal(barrier, inc=1, device_id=peer, device_id_type=MESH)

    near = [(me_r, col_at(b)) for b in (1, -1)]
    near += [(row_at(a), col_at(b)) for a in (1, -1) for b in (1, -1)]
    for peer in near:
        greet(0, peer)
    for_chips(greet)
    load.wait()

    peak = None
    for r in range(0, ny, SUBLANES):
        profiles = primitives([u[f, r : r + SUBLANES, :] for f in range(5)])
        speed = jnp.maximum(jnp.abs(profiles[1]), jnp.abs(profiles[2]))
        speed = speed + sound(profiles[0], profiles[4])
        for c in range(0, nx, LANES):
            part = speed[:, c : c + LANES]
            peak = part if peak is None else jnp.maximum(peak, part)
    peak = jnp.max(jnp.max(peak, axis=0, keepdims=True), axis=1, keepdims=True)
    mine[...] = jnp.broadcast_to(peak, mine.shape)

    lane = lax.broadcasted_iota(jnp.int32, (ny, LANES), 1)
    pack_r = pack_l = None
    for f in range(5):
        edge_r = pltpu.roll(u[f, 0:ny, nx - LANES : nx], 8 * f + 3, 1)
        edge_l = u[f, 0:ny, 0:LANES]
        if f:
            edge_l = pltpu.roll(edge_l, 8 * f, 1)
            pack_r = jnp.where(lane < 8 * f, pack_r, edge_r)
            pack_l = jnp.where(lane < 8 * f, pack_l, edge_l)
        else:
            pack_r, pack_l = edge_r, edge_l
    xr[...] = pack_r
    xl[...] = pack_l
    for f in range(5):
        yt[3 * f : 3 * f + 3, :] = u[f, 0:3, :]
        yb[3 * f : 3 * f + 3, :] = u[f, ny - 3 : ny, :]
    yt[15:16, :] = u[0, 0:1, :]
    yb[15:16, :] = u[0, 0:1, :]
    pl.semaphore_wait(barrier, count - 1 + len(near))
    pair = pltpu.make_async_remote_copy(
        src_ref=mine, dst_ref=theirs, send_sem=pair_send, recv_sem=pair_recv,
        device_id=partner, device_id_type=MESH,
    )
    pair.start()
    top, bottom = pl.ds(0, SUBLANES), pl.ds(ny - SUBLANES, SUBLANES)
    halos = []
    for i, (src, dst, device) in enumerate(
        [
            (yb, rya, (me_r, col_at(1))),
            (yt, ryb, (me_r, col_at(-1))),
            (xr, rxl, (row_at(1), me_c)),
            (xl, rxr, (row_at(-1), me_c)),
            (xr.at[bottom], rc.at[0], (row_at(1), col_at(1))),
            (xl.at[bottom], rc.at[1], (row_at(-1), col_at(1))),
            (xr.at[top], rc.at[2], (row_at(1), col_at(-1))),
            (xl.at[top], rc.at[3], (row_at(-1), col_at(-1))),
        ]
    ):
        halos.append(
            pltpu.make_async_remote_copy(
                src_ref=src, dst_ref=dst, send_sem=halo_send.at[i], recv_sem=halo_recv.at[i],
                device_id=device, device_id_type=MESH,
            )
        )
        halos[i].start()

    pair.wait_recv()
    both[...] = jnp.maximum(mine[...], theirs[...])

    def tell(d, peer):
        pltpu.make_async_remote_copy(
            src_ref=both, dst_ref=others.at[d - 1], send_sem=peak_send, recv_sem=peak_recv,
            device_id=peer, device_id_type=MESH,
        ).start()

    for_chips(tell)

    up, down = shifts(nx, 1)

    def sweep_tile(at):
        profiles = primitives([u[f, at, :] for f in range(5)])
        for f, difference in enumerate(flux_differences(profiles, up, down, 1)):
            df[f, at, :] = difference

    deep = 2 * SUBLANES if ny % (2 * SUBLANES) == 0 else SUBLANES

    @pl.loop(0, ny // deep)
    def _(tile):
        sweep_tile(pl.ds(pl.multiple_of(tile * deep, deep), deep))

    halos[0].wait_recv()
    halos[1].wait_recv()
    for f in range(5):
        u[f, ny : ny + 3, :] = ryb[3 * f : 3 * f + 3, :]
        u[f, ny + 3 : ny + 5, :] = u[f, 3:5, :]
        u[f, ny + 5 : ny + 8, :] = rya[3 * f : 3 * f + 3, :]
    sweep_tile(pl.ds(ny, SUBLANES))

    for copy in halos[2:]:
        copy.wait_recv()
    total = ny + SUBLANES
    lane = lax.broadcasted_iota(jnp.int32, (total, LANES), 1)
    below = lax.broadcasted_iota(jnp.int32, (SUBLANES, LANES), 0) < 4
    far_left = jnp.concatenate([rxl[...], jnp.where(below, rc[2], rc[0])], axis=0)
    far_right = jnp.concatenate([rxr[...], jnp.where(below, rc[3], rc[1])], axis=0)
    seam = []
    for f in range(5):
        begin = u[f, :, 0:LANES]
        end = pltpu.roll(u[f, :, nx - LANES : nx], 64, 1)
        before = pltpu.roll(far_left, 125 - 8 * f, 1)
        after = pltpu.roll(far_right, 64 - 8 * f, 1)
        tile = jnp.where(lane < 32, begin, end)
        tile = jnp.where(lane >= 125, before, tile)
        seam.append(jnp.where((lane >= 64) & (lane < 67), after, tile))
    profiles = primitives(seam)
    up, down = shifts(LANES, 1)
    for f, difference in enumerate(flux_differences(profiles, up, down, 1)):
        df[f, :, 0:LANES] = jnp.where(lane < 3, difference, df[f, :, 0:LANES])
        df[f, :, nx - LANES : nx] = jnp.where(
            lane >= 125, pltpu.roll(difference, 64, 1), df[f, :, nx - LANES : nx]
        )

    pltpu.make_async_copy(others, others, peak_recv).wait()
    peak = jnp.maximum(both[...], jnp.max(others[...], axis=0))
    half_step = (0.5 * COURANT) / peak

    up, down = shifts(total, 0)

    wide = 2 * LANES if nx % (2 * LANES) == 0 else LANES
    half_step = jnp.concatenate([half_step] * (wide // LANES), axis=1)

    @pl.loop(0, nx // wide)
    def _(chunk):
        at = pl.ds(pl.multiple_of(chunk * wide, wide), wide)
        cells = [u[f, :, at] - half_step * df[f, :, at] for f in range(5)]
        profiles = primitives(cells)
        for f, difference in enumerate(flux_differences(profiles, up, down, 2)):
            result = cells[f] - half_step * difference
            out[f, 0, :, at] = result[0:ny]

    for copy in halos:
        copy.wait_send()
    pair.wait_send()
    pltpu.make_async_copy(others, others, peak_send).wait()


def local(rows, cols, fields):
    ny, nx = fields.shape[2], fields.shape[3]
    vmem = lambda *shape: pltpu.VMEM(shape, jnp.float32)
    dma = pltpu.SemaphoreType.DMA
    return pl.pallas_call(
        functools.partial(kernel, rows, cols),
        out_shape=jax.ShapeDtypeStruct(fields.shape, fields.dtype),
        in_specs=[pl.BlockSpec(memory_space=pltpu.HBM)],
        out_specs=pl.BlockSpec(memory_space=pltpu.VMEM),
        scratch_shapes=[
            vmem(5, ny + SUBLANES, nx),
            vmem(5, ny + SUBLANES, nx),
            vmem(ny, LANES),
            vmem(ny, LANES),
            vmem(16, nx),
            vmem(16, nx),
            vmem(ny, LANES),
            vmem(ny, LANES),
            vmem(16, nx),
            vmem(16, nx),
            vmem(4, SUBLANES, LANES),
            vmem(1, LANES),
            vmem(1, LANES),
            vmem(1, LANES),
            vmem(rows * cols // 2 - 1, 1, LANES),
            dma,
            dma((8,)),
            dma((8,)),
            dma,
            dma,
            dma,
            dma,
        ],
        compiler_params=pltpu.CompilerParams(
            collective_id=0, has_side_effects=True, vmem_limit_bytes=55072 * 1024
        ),
        name="sweeps",
    )(fields)


def solution(mesh):
    spec = P(None, None, "col", "row")
    return jax.shard_map(
        functools.partial(local, mesh.shape["row"], mesh.shape["col"]),
        mesh=mesh,
        in_specs=(spec,),
        out_specs=spec,
        check_vma=False,
    )
```
